256 devices in a mesh: tile: 64 (over y, z, core), head: 4 (over x).
Axes of the slice: x: 4, y: 4, z: 8, core: 2. Of those that a mesh axis runs over, the one named last changes fastest.
Arguments:
- tokens: bfloat16 [256, 262144], P('head', 'tile'), may hold values from -6 to 6
- grad_in: bfloat16 [256, 262144], P('head', 'tile'), may hold values from -6 to 6
- w_qkv: bfloat16 [3, 256, 256], P(None, 'head'), may hold values from -0.375 to 0.375
- w_out: bfloat16 [256, 256], P('head'), may hold values from -0.375 to 0.375
- neighbors: int32 [9, 262144], P(None, 'tile'), may hold values from 0 to 4479, as said below
- send_rows: int32 [64, 3, 128], P('tile'), may hold values from 0 to 4096, as said below
Outputs:
- d_tokens: float32 [256, 262144], P('head', 'tile')
- grad_qkv: float32 [3, 256, 256], P(None, 'head')
- grad_out: float32 [256, 256], P('head')
The draws below stay inside these ranges and needn't reach their ends.
Inputs may be any that keep to these rules, and one draw needn't show every extreme that they name: `send_rows`: entries of list p of index d are rows of index d, live entries first, the rest equal to 4096; list 2 of every index is full, and list 0 of index 0 is half full. `neighbors`: slot 0 of row r of an index is r itself; an entry below 4096 lies within 64 rows of r, counted around the index's 4096 rows; every entry at or above 4096 points to a live entry of the list it names.
All inputs are finite; a program needn't handle non-finite values.
Results may differ from the reference program's by a relative error of at most 0.0059.
Values may be sent and summed in bfloat16 or wider, within the bound.
No kernel may reach another device: no remote copies, remote signals or barrier semaphores. Data moves between devices by JAX's collectives and lax.ppermute only.
A program may use at most 64 MiB of HBM per device.

```python
import math
import jax
import jax.numpy as jnp
from jax import lax

C = 256
HEADS = 8
NBR = 9
ROWS_DEV = 4096
BORDER = 128
GROUPS = 64
ROWS = 262144


def border_counts(key):
    counts = jax.random.randint(jax.random.fold_in(key, 11), (GROUPS, 3), BORDER // 2, BORDER + 1)
    counts = counts.at[:, 2].set(BORDER)
    counts = counts.at[0, 0].set(BORDER // 2)
    return counts.astype(jnp.int32)


def draw_send_rows(key, part):
    counts = border_counts(key)
    subkeys = jax.random.split(jax.random.fold_in(key, 23), GROUPS * 3)
    chosen = jax.vmap(lambda subkey: jax.random.permutation(subkey, ROWS_DEV)[:BORDER])(subkeys)
    chosen = chosen.reshape(GROUPS, 3, BORDER)
    column = jnp.arange(BORDER, dtype=jnp.int32)
    return jnp.where(column[None, None, :] < counts[:, :, None], chosen, ROWS_DEV).astype(jnp.int32)


def draw_neighbors(key, part):
    counts = border_counts(key)
    first, second, third, fourth = jax.random.split(jax.random.fold_in(key, 37), 4)
    shape = (NBR - 1, GROUPS, ROWS_DEV)
    row_ids = jnp.arange(ROWS_DEV, dtype=jnp.int32)
    local = (row_ids[None, None, :] + jax.random.randint(first, shape, -64, 65)) % ROWS_DEV
    peer = jax.random.randint(second, shape, 0, 3)
    device = jnp.arange(GROUPS, dtype=jnp.int32)[None, :, None]
    offsets = jnp.array([1, GROUPS - 1, GROUPS // 2], dtype=jnp.int32)
    source = (device - offsets[peer]) % GROUPS
    live = counts[source, peer]
    column = jax.random.randint(third, shape, 0, BORDER) % live
    remote = ROWS_DEV + peer * BORDER + column
    picked = jax.random.randint(fourth, shape, 0, 8) == 0
    entries = jnp.where(picked, remote, local)
    entries = entries.at[NBR - 2, :, 0].set(ROWS_DEV + 3 * BORDER - 1)
    selfrow = jnp.broadcast_to(row_ids[None, None, :], (1, GROUPS, ROWS_DEV))
    whole = jnp.concatenate([selfrow, entries], axis=0)
    return whole.reshape(NBR, GROUPS * ROWS_DEV).astype(jnp.int32)


def block_levels(stream_key, extent, pieces, low, largest):
    loudness, own = 1.0, jax.random.fold_in(stream_key, 6)
    for dim, parts in pieces:
        heights = jnp.exp(jax.random.uniform(jax.random.fold_in(own, dim), (parts,), jnp.float32, low / len(pieces), largest / len(pieces)))
        loudness = loudness * jnp.repeat(heights, extent[dim] // parts).reshape([-1 if axis == dim else 1 for axis in range(len(extent))])
    return loudness


def gaussian(stream_key, shape, width, limit, shards=(), kind=jnp.bfloat16):
    level = block_levels(stream_key, shape, shards, -0.22, 0.18) if shards else 1.0
    values = jax.random.normal(stream_key, shape, jnp.float32) * width * level
    return jnp.minimum(jnp.maximum(values, -limit), limit).astype(kind)


def setup_inputs(seed: int = 0) -> dict:
    streams_of = jax.random.split(jax.random.key(seed), 7)
    return {
        "tokens": gaussian(streams_of[0], (C, ROWS), 1.0, 6.0, ((0, 4), (1, 64))),
        "grad_in": gaussian(streams_of[1], (C, ROWS), 1.0, 6.0, ((0, 4), (1, 64))),
        "w_qkv": gaussian(streams_of[2], (3, C, C), C ** -0.5, 0.375, ((1, 4),)),
        "w_out": gaussian(streams_of[3], (C, C), C ** -0.5, 0.375, ((0, 4),)),
        "neighbors": draw_neighbors(jax.random.fold_in(streams_of[6], 71), 0),
        "send_rows": draw_send_rows(jax.random.fold_in(streams_of[6], 71), 0),
    }


def reference(tokens, grad_in, w_qkv, w_out, neighbors, send_rows):
    total_rows = GROUPS * ROWS_DEV
    head_dim = C // HEADS
    score_scale = 1.0 / math.sqrt(head_dim)
    devices = jnp.arange(GROUPS, dtype=jnp.int32)
    offsets = jnp.array([1, GROUPS - 1, GROUPS // 2], dtype=jnp.int32)
    sources = (devices[:, None] - offsets[None, :]) % GROUPS
    lists = send_rows[sources, jnp.arange(3, dtype=jnp.int32)[None, :], :]
    remote = jnp.where(lists < ROWS_DEV, sources[:, :, None] * ROWS_DEV + lists, total_rows).astype(jnp.int32)
    own_rows = devices[:, None] * ROWS_DEV + jnp.arange(ROWS_DEV, dtype=jnp.int32)[None, :]
    mapping = jnp.concatenate([own_rows, remote.reshape(GROUPS, 3 * BORDER)], axis=1)
    local_table = neighbors.reshape(NBR, GROUPS, ROWS_DEV)
    table = mapping[devices[None, :, None], local_table].reshape(NBR, total_rows).astype(jnp.int32)
    x_rows = tokens.T
    dy_rows = grad_in.T
    query = jnp.dot(x_rows, w_qkv[0].T, preferred_element_type=jnp.float32).astype(jnp.bfloat16)
    keys = jnp.dot(x_rows, w_qkv[1].T, preferred_element_type=jnp.float32).astype(jnp.bfloat16)
    values = jnp.dot(x_rows, w_qkv[2].T, preferred_element_type=jnp.float32).astype(jnp.bfloat16)
    packed = jnp.concatenate([keys, values], axis=1)
    padded = jnp.concatenate([packed, jnp.zeros((1, 2 * C), jnp.bfloat16)], axis=0)
    grad_att = jnp.dot(dy_rows, w_out.T, preferred_element_type=jnp.float32)

    def block_step(totals, block_index):
        start = (block_index * ROWS_DEV).astype(jnp.int32)
        picks = lax.dynamic_slice_in_dim(table, start, ROWS_DEV, 1)
        near = padded[picks].astype(jnp.float32)
        near_keys = near[:, :, :C].reshape(NBR, ROWS_DEV, HEADS, head_dim)
        near_values = near[:, :, C:].reshape(NBR, ROWS_DEV, HEADS, head_dim)
        query_rows = lax.dynamic_slice_in_dim(query, start, ROWS_DEV, 0).astype(jnp.float32).reshape(ROWS_DEV, HEADS, head_dim)
        dout_rows = lax.dynamic_slice_in_dim(grad_att, start, ROWS_DEV, 0).reshape(ROWS_DEV, HEADS, head_dim)
        scores = jnp.einsum('rhd,jrhd->jrh', query_rows, near_keys) * score_scale
        expon = jnp.exp(scores)
        probs = expon / lax.optimization_barrier(jnp.sum(expon, axis=0))
        attended = jnp.einsum('jrh,jrhd->rhd', probs, near_values)
        dprob = jnp.einsum('rhd,jrhd->jrh', dout_rows, near_values)
        dscore = probs * (dprob - lax.optimization_barrier(jnp.sum(probs * dprob, axis=0)))
        grad_query = jnp.einsum('jrh,jrhd->rhd', dscore, near_keys) * score_scale
        grad_keys = dscore[..., None] * query_rows[None] * score_scale
        grad_values = probs[..., None] * dout_rows[None]
        grad_near = jnp.concatenate([grad_keys.reshape(NBR, ROWS_DEV, C), grad_values.reshape(NBR, ROWS_DEV, C)], axis=2)
        totals = totals.at[picks.reshape(-1)].add(grad_near.reshape(NBR * ROWS_DEV, 2 * C))
        return (totals, (attended.reshape(ROWS_DEV, C).astype(jnp.bfloat16), grad_query.reshape(ROWS_DEV, C)))
    totals, (attended, grad_query) = lax.scan(block_step, jnp.zeros((total_rows + 1, 2 * C), jnp.float32), jnp.arange(GROUPS, dtype=jnp.int32))
    attended = attended.reshape(total_rows, C)
    grad_q = grad_query.reshape(total_rows, C).astype(jnp.bfloat16)
    grad_k = totals[:total_rows, :C].astype(jnp.bfloat16)
    grad_v = totals[:total_rows, C:].astype(jnp.bfloat16)
    d_rows = dy_rows.astype(jnp.float32) + jnp.dot(grad_q, w_qkv[0], preferred_element_type=jnp.float32) + jnp.dot(grad_k, w_qkv[1], preferred_element_type=jnp.float32) + jnp.dot(grad_v, w_qkv[2], preferred_element_type=jnp.float32)
    grad_scale = 1.0 / math.sqrt(total_rows)
    grad_qkv = jnp.stack([jnp.dot(grad_q.T, x_rows, preferred_element_type=jnp.float32), jnp.dot(grad_k.T, x_rows, preferred_element_type=jnp.float32), jnp.dot(grad_v.T, x_rows, preferred_element_type=jnp.float32)]) * grad_scale
    grad_out = jnp.dot(attended.T, dy_rows, preferred_element_type=jnp.float32) * grad_scale
    return (d_rows.T, grad_qkv, grad_out)
```

```python
import math

import jax
import jax.numpy as jnp
from jax import lax
from jax.experimental import pallas as pl
from jax.experimental.pallas import tpu as pltpu
from jax.sharding import PartitionSpec as P

C = 256
HEADS = 8
NBR = 9
HEAD_DIM = 32
BLOCK = 128
SIDE = 64
WINDOW = BLOCK + 2 * SIDE
LOG2E = math.log2(math.e)
F32 = jnp.float32
BF16 = jnp.bfloat16


def passed_along(value, axis, steps):
    count = lax.axis_size(axis)
    pairs = [(source, (source + steps) % count) for source in range(count)]
    return lax.ppermute(value, axis, pairs)


def grouped(value, groups):
    return lax.all_to_all(value, "tile", 0, 0, axis_index_groups=groups)


def vmem_spec():
    return pl.BlockSpec(memory_space=pltpu.VMEM)


def smem_spec():
    return pl.BlockSpec(memory_space=pltpu.SMEM)


def nt(a, b):
    return lax.dot_general(a, b, (((1,), (1,)), ((), ())), preferred_element_type=F32)


def tn(a, b):
    return lax.dot_general(a, b, (((0,), (0,)), ((), ())), preferred_element_type=F32)


def nn(a, b):
    return jnp.dot(a, b, preferred_element_type=F32)


def one_hot_rows(lists, start, count):
    rows = lax.broadcasted_iota(jnp.int32, (count, lists.shape[1]), 0) + start
    return jnp.where(rows == lists, 1.0, 0.0).astype(BF16)


def prepare(place, tokens, grad_in, w_qkv, w_out, lists, out0, out1, out2, out3, halo, padded):
    head = place[0]
    rows = tokens.shape[1]
    own = rows // 4
    ext = own + 2 * SIDE
    shifted = pltpu.roll(tokens[...].astype(F32), SIDE, 1).astype(BF16)
    padded[:, :rows] = shifted
    padded[:, rows:] = shifted[:, : 2 * SIDE]
    for step, out in enumerate((out0, out1, out2, out3)):
        target = (head + step) & 3
        first = pl.multiple_of(target * own, own)
        out[:, :ext] = padded[:, pl.ds(first, ext)]
        out[:, ext : ext + own] = grad_in[:, pl.ds(first, own)]
        base = ext + own
        for kind in range(3):
            out[:, base + kind * C : base + (kind + 1) * C] = w_qkv[kind]
        out[:, base + 3 * C :] = w_out[...]
    chosen = jnp.zeros(halo.shape, F32)
    for start in range(0, rows, 512):
        chosen = chosen + nn(tokens[:, start : start + 512], one_hot_rows(lists[...], start, 512))
    halo[...] = chosen.astype(BF16)


def attend(
    place, c0, c1, c2, c3, h0, h1, h2, h3, neighbors, o0, o1, o2, o3,
    xe, dy, wq, wkv, wo, qs, ds, kvt, kv, dkv, da, dkvt, grads, summed, bias,
):
    head = place[0]
    own = dy.shape[1]
    ext = own + 2 * SIDE
    full = xe.shape[1]
    border = full - ext
    cand = WINDOW + border
    rows_all = neighbors.shape[1]
    scale = 1.0 / math.sqrt(HEAD_DIM)
    wq[...] = jnp.zeros_like(wq)
    wo[...] = jnp.zeros_like(wo)
    for step, (chunk, far) in enumerate(((c0, h0), (c1, h1), (c2, h2), (c3, h3))):
        source = (head - step + 4) & 3
        row = pl.multiple_of(source * 64, 64)
        xe[pl.ds(row, 64), :ext] = chunk[:, :ext]
        xe[pl.ds(row, 64), ext:] = far[...]
        dy[pl.ds(row, 64), :] = chunk[:, ext : ext + own]
        base = ext + own
        for k in range(2):
            dest = pl.multiple_of(source * 128 + 64 * k, 64)
            part = slice(32 * k, 32 * k + 32)
            wq[pl.ds(dest, 32), :] = chunk[part, base : base + C]
            wkv[pl.ds(dest, 32), :] = chunk[part, base + C : base + 2 * C]
            wkv[pl.ds(dest + 32, 32), :] = chunk[part, base + 2 * C : base + 3 * C]
            wo[pl.ds(dest + 32, 32), :] = chunk[part, base + 3 * C :]
    for start in range(0, full, 128):
        cols = slice(start, start + 128)
        block = nn(wkv[...], xe[:, cols]).astype(BF16)
        kvt[:, cols] = block
        kv[cols, :] = block.T
    for start in range(0, ext, 128):
        cols = slice(start, start + 128)
        qs[cols, :] = nn(wq[...], xe[:, cols]).astype(BF16).T
    for start in range(0, own, 128):
        cols = slice(start, start + 128)
        ds[cols, :] = nn(wo[...], dy[:, cols]).astype(BF16).T
    dkv[...] = jnp.zeros_like(dkv)
    da[:, own:] = jnp.zeros((2 * C, 2 * SIDE), F32)
    lane_head = lax.broadcasted_iota(jnp.int32, (BLOCK, C), 1) // 64

    def step(b, carry):
        first = pl.multiple_of(b * BLOCK, BLOCK)
        near = neighbors[:, pl.ds(pl.multiple_of(head * own + b * BLOCK, BLOCK), BLOCK)]
        shifted = (near - (head * own + b * BLOCK - SIDE)) & (rows_all - 1)
        index = jnp.where(near < rows_all, shifted, near - rows_all + WINDOW)
        for start in range(0, cand, 128):
            rows = lax.broadcasted_iota(jnp.int32, (128, BLOCK), 0) + start
            count = jnp.zeros((128, BLOCK), F32)
            for slot in range(NBR):
                count = count + jnp.where(rows == index[slot : slot + 1, :], 1.0, 0.0)
            bias[start : start + 128, :] = jnp.where(count > 0.5, jnp.log(count) * LOG2E, -1e30)
        for g in range(2):
            cols = slice(C * g, C * g + C)
            query = qs[pl.ds(first + SIDE, BLOCK), cols]
            dout = ds[pl.ds(first, BLOCK), cols]
            both = jnp.concatenate([kv[pl.ds(first, WINDOW), cols], kv[ext:, cols]], axis=0)
            total = jnp.zeros((cand, C), F32)
            zero = jnp.zeros((BLOCK, C), BF16)
            for hh in range(4):
                mine = lane_head == hh
                stacked = jnp.concatenate(
                    [jnp.where(mine, query, zero), jnp.where(mine, dout, zero)], axis=0
                )
                products = nt(both, stacked)
                expon = jnp.exp2(products[:, :BLOCK] * (scale * LOG2E) + bias[...])
                dprob = products[:, BLOCK:]
                inverse = 1.0 / jnp.sum(expon, axis=0, keepdims=True)
                mean = jnp.sum(expon * dprob, axis=0, keepdims=True) * inverse
                prob = expon * inverse
                dscore = prob * (dprob - mean)
                weights = jnp.concatenate([dscore.astype(BF16), prob.astype(BF16)], axis=1)
                total = total + nn(weights, stacked)
                top = C * g + 64 * hh
                pair = jnp.concatenate(
                    [kvt[top : top + 64, pl.ds(first, WINDOW)], kvt[top : top + 64, ext:]], axis=1
                )
                result = nn(pair, weights)
                da[top : top + 32, pl.ds(first, BLOCK)] = result[:32, :BLOCK] * scale
                da[top + 32 : top + 64, pl.ds(first, BLOCK)] = result[32:, BLOCK:]
            dkv[pl.ds(first, WINDOW), cols] += total[:WINDOW]
            dkv[ext:, cols] += total[WINDOW:]
        return carry

    lax.fori_loop(0, own // BLOCK, step, 0)
    col_scale = jnp.where((lax.broadcasted_iota(jnp.int32, (128, 2 * C), 1) & 63) < 32, scale, 1.0)
    for start in range(0, full, 128):
        rows = slice(start, start + 128)
        dkvt[:, rows] = (dkv[rows, :] * col_scale).astype(BF16).T
    own_grads = pltpu.roll(da[...], SIDE, 1).astype(BF16)
    summed[:, :ext] = (tn(wkv[...], dkvt[:, :ext]) + tn(wq[...], own_grads)).astype(BF16)
    summed[:, ext:] = tn(wkv[...], dkvt[:, ext:]).astype(BF16)
    grads[0] = nt(own_grads, xe[:, :ext]).astype(BF16)
    grads[1] = nt(dkvt[...], xe[...]).astype(BF16)
    grads[2] = nt(da[:, :own].astype(BF16), dy[...]).astype(BF16)
    for step_out, out in enumerate((o0, o1, o2, o3)):
        target = (head + step_out) & 3
        out[:, :full] = summed[pl.ds(pl.multiple_of(target * 64, 64), 64), :]
        for k in range(2):
            top = pl.multiple_of(target * 128 + 64 * k, 64)
            part = slice(32 * k, 32 * k + 32)
            out[part, full : full + C] = grads[0, pl.ds(top, 32), :]
            out[part, full + C : full + 2 * C] = grads[1, pl.ds(top, 32), :]
            out[part, full + 2 * C : full + 3 * C] = grads[1, pl.ds(top + 32, 32), :]
            out[part, full + 3 * C :] = grads[2, pl.ds(top + 32, 32), :]


def add_up(r0, r1, r2, r3, b0, b1, b2, total):
    border = b0.shape[1]
    full = r0.shape[1] - 4 * C
    first = full - 3 * border
    parts = (r0, r1, r2, r3)
    for peer, out in enumerate((b0, b1, b2)):
        cols = slice(first + peer * border, first + (peer + 1) * border)
        out[...] = sum(part[:, cols].astype(F32) for part in parts).astype(BF16)
    for kind in range(4):
        cols = slice(full + kind * C, full + (kind + 1) * C)
        rows = slice(kind * 64, kind * 64 + 64)
        total[rows, :] = sum(part[:, cols].astype(F32) for part in parts).astype(BF16)


def finish(place, r0, r1, r2, r3, b0, b1, b2, grad_in, lists, out, padded):
    head = place[0]
    rows = grad_in.shape[1]
    own = rows // 4
    ext = own + 2 * SIDE
    padded[...] = jnp.zeros_like(padded)
    for step, part in enumerate((r0, r1, r2, r3)):
        source = (head - step + 4) & 3
        first = pl.multiple_of(source * own, own)
        padded[:, pl.ds(first, ext)] += part[:, :ext].astype(F32)
    padded[:, : 2 * SIDE] += padded[:, rows:]
    aligned = pltpu.roll(padded[:, :rows], rows - SIDE, 1)
    back = jnp.concatenate([b0[...], b1[...], b2[...]], axis=1)
    for start in range(0, rows, 512):
        cols = slice(start, start + 512)
        returned = nt(back, one_hot_rows(lists[...], start, 512))
        out[:, cols] = grad_in[:, cols].astype(F32) + aligned[:, cols] + returned


def kernel_call(body, out_shape, inputs, scratch=(), mib=48):
    specs = [smem_spec() if value.dtype == jnp.int32 and value.size == 1 else vmem_spec() for value in inputs]
    outs = [vmem_spec() for _ in out_shape] if isinstance(out_shape, (list, tuple)) else vmem_spec()
    return pl.pallas_call(
        body,
        out_shape=out_shape,
        in_specs=specs,
        out_specs=outs,
        scratch_shapes=list(scratch),
        compiler_params=pltpu.CompilerParams(vmem_limit_bytes=mib * 1024 * 1024),
    )(*inputs)


def sds(shape, dtype):
    return jax.ShapeDtypeStruct(shape, dtype)


def local(tokens, grad_in, w_qkv, w_out, neighbors, send_rows):
    groups = lax.axis_size("tile")
    border = send_rows.shape[2]
    offsets = (1, groups - 1, groups // 2)
    rows = tokens.shape[1]
    own = rows // 4
    ext = own + 2 * SIDE
    full = ext + 3 * border
    cand = WINDOW + 3 * border
    place = lax.axis_index("head").reshape(1).astype(jnp.int32)
    lists = send_rows.reshape(1, 3 * border)
    width = ext + own + 4 * C

    with jax.named_scope("prepare"):
        *chunks, halo = kernel_call(
            prepare,
            [sds((64, width), BF16)] * 4 + [sds((64, 3 * border), BF16)],
            (place, tokens, grad_in, w_qkv, w_out, lists),
            [pltpu.VMEM((64, rows + 2 * SIDE), BF16)],
        )
    with jax.named_scope("border_rows"):
        mine = jnp.concatenate(
            [
                passed_along(halo[:, peer * border : (peer + 1) * border], "tile", offsets[peer])
                for peer in range(3)
            ],
            axis=1,
        )
        far = [mine] + [passed_along(mine, "head", step) for step in (1, 2, 3)]
    with jax.named_scope("exchange"):
        chunks = [chunks[0]] + [passed_along(chunks[step], "head", step) for step in (1, 2, 3)]
    with jax.named_scope("attention"):
        parts = kernel_call(
            attend,
            [sds((64, full + 4 * C), BF16)] * 4,
            (place, *chunks, *far, neighbors),
            [
                pltpu.VMEM((C, full), BF16),
                pltpu.VMEM((C, own), BF16),
                pltpu.VMEM((2 * C, C), BF16),
                pltpu.VMEM((2 * C, C), BF16),
                pltpu.VMEM((2 * C, C), BF16),
                pltpu.VMEM((ext, 2 * C), BF16),
                pltpu.VMEM((own, 2 * C), BF16),
                pltpu.VMEM((2 * C, full), BF16),
                pltpu.VMEM((full, 2 * C), BF16),
                pltpu.VMEM((full, 2 * C), F32),
                pltpu.VMEM((2 * C, ext), F32),
                pltpu.VMEM((2 * C, full), BF16),
                pltpu.VMEM((3, 2 * C, C), BF16),
                pltpu.VMEM((C, full), BF16),
                pltpu.VMEM((cand, BLOCK), F32),
            ],
        )
    with jax.named_scope("return"):
        parts = [parts[0]] + [passed_along(parts[step], "head", step) for step in (1, 2, 3)]
        *back, total = kernel_call(
            add_up,
            [sds((64, border), BF16)] * 3 + [sds((C, C), BF16)],
            tuple(parts),
        )
        back = [
            passed_along(back[peer], "tile", (groups - offsets[peer]) % groups)
            for peer in range(3)
        ]
        d_tokens = kernel_call(
            finish,
            sds((64, rows), F32),
            (place, *parts, *back, grad_in, lists),
            [pltpu.VMEM((64, rows + 2 * SIDE), F32)],
        )
    with jax.named_scope("weight_sums"):
        near = [[16 * y + 2 * z + c for y in range(4) for c in range(2)] for z in range(8)]
        line = [[16 * y + 2 * z + c for z in range(8)] for y in range(4) for c in range(2)]
        piece = (8, C // 8, C)
        value = grouped(total.reshape(piece), near)
        value = value.astype(F32).sum(0).astype(BF16)
        value = grouped(jnp.broadcast_to(value[None], piece), line)
        value = value.astype(F32).sum(0).astype(BF16)
        value = grouped(jnp.broadcast_to(value[None], piece), near)
        grad_scale = 1.0 / math.sqrt(rows * groups)
        value = value.reshape(4, 64, C).astype(F32) * grad_scale
    return (d_tokens, value[:3], value[3])


def solution(mesh):
    return jax.shard_map(
        local,
        mesh=mesh,
        in_specs=(
            P("head", "tile"),
            P("head", "tile"),
            P(None, "head", None),
            P("head", None),
            P(None, "tile"),
            P("tile", None, None),
        ),
        out_specs=(P("head", "tile"), P(None, "head", None), P("head", None)),
        check_vma=False,
    )
```

```python
import math

import jax
import jax.numpy as jnp
from jax import lax
from jax.experimental import pallas as pl
from jax.experimental.pallas import tpu as pltpu
from jax.sharding import PartitionSpec as P

C = 256
HEADS = 8
NBR = 9
HEAD_DIM = 32
BLOCK = 128
SIDE = 64
CHUNK = 128
WINDOW = BLOCK + 2 * SIDE
LOG2E = math.log2(math.e)
F32 = jnp.float32
BF16 = jnp.bfloat16


def passed_along(value, axis, steps):
    count = lax.axis_size(axis)
    pairs = [(source, (source + steps) % count) for source in range(count)]
    return lax.ppermute(value, axis, pairs)


def grouped(value, groups):
    return lax.all_to_all(value, "tile", 0, 0, axis_index_groups=groups)


def plates(heads):
    return [
        [(16 * y + 2 * z + c) * heads + h for h in range(heads) for y in range(4) for c in range(2)]
        for z in range(8)
    ]


def vmem_spec():
    return pl.BlockSpec(memory_space=pltpu.VMEM)


def nt(a, b):
    return lax.dot_general(a, b, (((1,), (1,)), ((), ())), preferred_element_type=F32)


def tn(a, b):
    return lax.dot_general(a, b, (((0,), (0,)), ((), ())), preferred_element_type=F32)


def nn(a, b):
    return jnp.dot(a, b, preferred_element_type=F32)


def one_hot_rows(lists, start, count):
    rows = lax.broadcasted_iota(jnp.int32, (count, lists.shape[1]), 0) + start
    return jnp.where(rows == lists, 1.0, 0.0).astype(BF16)


def choose(tokens, lists, halo, x, sems):
    rows = tokens.shape[1]
    quarter = rows // 4
    fetches = [
        pltpu.make_async_copy(
            tokens.at[:, pl.ds(part * quarter, quarter)],
            x.at[:, pl.ds(part * quarter, quarter)],
            sems.at[part],
        )
        for part in range(4)
    ]
    for fetch in fetches:
        fetch.start()
    chosen = jnp.zeros(halo.shape, F32)
    for part, fetch in enumerate(fetches):
        fetch.wait()
        for start in range(part * quarter, (part + 1) * quarter, 512):
            chosen = chosen + nn(x[:, start : start + 512], one_hot_rows(lists[...], start, 512))
    halo[...] = chosen.astype(BF16)


def prepare(
    place, tokens, grad_in, w_qkv, w_out, halo, out0, out1, out2, out3, x, wv, wo, padded, sems
):
    head = place[0]
    rows = tokens.shape[1]
    own = rows // 4
    ext = own + 2 * SIDE
    base = ext + own
    outs = (out0, out1, out2, out3)
    fetch_x = pltpu.make_async_copy(tokens, x, sems.at[0])
    fetch_v = pltpu.make_async_copy(w_qkv, wv, sems.at[1])
    fetch_o = pltpu.make_async_copy(w_out, wo, sems.at[2])
    fetches = [
        pltpu.make_async_copy(
            grad_in.at[:, pl.ds(pl.multiple_of(((head + step) & 3) * own, own), own)],
            out.at[:, pl.ds(ext, own)],
            sems.at[3 + step],
        )
        for step, out in enumerate(outs)
    ]
    fetch_x.start()
    fetch_v.start()
    fetch_o.start()
    for fetch in fetches:
        fetch.start()
    fetch_x.wait()
    shifted = pltpu.roll(x[...].astype(F32), SIDE, 1).astype(BF16)
    padded[:, :rows] = shifted
    padded[:, rows:] = shifted[:, : 2 * SIDE]
    for step, out in enumerate(outs):
        first = pl.multiple_of(((head + step) & 3) * own, own)
        out[:, :ext] = padded[:, pl.ds(first, ext)]
    fetch_v.wait()
    fetch_o.wait()
    for out in outs:
        for kind in range(3):
            out[:, base + kind * C : base + (kind + 1) * C] = wv[kind]
        out[:, base + 3 * C :] = wo[...]
    for fetch in fetches:
        fetch.wait()


def attend(
    place, c0, c1, c2, c3, far, neighbors, o0, o1, o2, o3, sums,
    xe, dy, wq, wkv, wo, qs, ds, kvt, kv, dkv, da, dkvt, grads, summed, bias,
    products0, products1, weights0, weights1,
):
    head = place[0]
    own = dy.shape[1]
    ext = own + 2 * SIDE
    full = xe.shape[1]
    border = full - ext
    cand = WINDOW + border
    rows_all = neighbors.shape[1]
    scale = 1.0 / math.sqrt(HEAD_DIM)
    wq[...] = jnp.zeros_like(wq)
    wo[...] = jnp.zeros_like(wo)
    xe[:, ext:] = far[...].reshape(C, border)
    for step, chunk in enumerate((c0, c1, c2, c3)):
        source = (head - step + 4) & 3
        row = pl.multiple_of(source * 64, 64)
        xe[pl.ds(row, 64), :ext] = chunk[:, :ext]
        dy[pl.ds(row, 64), :] = chunk[:, ext : ext + own]
        base = ext + own
        for k in range(2):
            dest = pl.multiple_of(source * 128 + 64 * k, 64)
            part = slice(32 * k, 32 * k + 32)
            wq[pl.ds(dest, 32), :] = chunk[part, base : base + C]
            wkv[pl.ds(dest, 32), :] = chunk[part, base + C : base + 2 * C]
            wkv[pl.ds(dest + 32, 32), :] = chunk[part, base + 2 * C : base + 3 * C]
            wo[pl.ds(dest + 32, 32), :] = chunk[part, base + 3 * C :]
    for start in range(0, full, 128):
        cols = slice(start, start + 128)
        block = nn(wkv[...], xe[:, cols]).astype(BF16)
        kvt[:, cols] = block
        kv[cols, :] = block.T
    for start in range(0, ext, 128):
        cols = slice(start, start + 128)
        qs[cols, :] = nn(wq[...], xe[:, cols]).astype(BF16).T
    for start in range(0, own, 128):
        cols = slice(start, start + 128)
        ds[cols, :] = nn(wo[...], dy[:, cols]).astype(BF16).T
    dkv[...] = jnp.zeros_like(dkv)
    da[:, own:] = jnp.zeros((2 * C, 2 * SIDE), F32)
    lane_head = lax.broadcasted_iota(jnp.int32, (BLOCK, C), 1) // 64

    zero = jnp.zeros((BLOCK, C), BF16)
    last = own // BLOCK - 1

    def operands(b, g, hh):
        first = pl.multiple_of(b * BLOCK, BLOCK)
        cols = slice(C * g, C * g + C)
        mine = lane_head == hh
        query = jnp.where(mine, qs[pl.ds(first + SIDE, BLOCK), cols], zero)
        dout = jnp.where(mine, ds[pl.ds(first, BLOCK), cols], zero)
        return jnp.concatenate([query, dout], axis=0)

    def multiply(b, g, hh, products):
        first = pl.multiple_of(b * BLOCK, BLOCK)
        cols = slice(C * g, C * g + C)
        out = slice(C * hh, C * hh + C)
        both = jnp.concatenate([kv[pl.ds(first, WINDOW), cols], kv[ext:, cols]], axis=0)
        products[:, out] = nt(both, operands(b, g, hh))

    def weigh(hh, products, weights):
        left = slice(C * hh, C * hh + BLOCK)
        right = slice(C * hh + BLOCK, C * hh + C)
        acc = jnp.zeros((8, BLOCK), F32)
        for start in range(0, cand, CHUNK):
            rows = slice(start, start + CHUNK)
            expon = jnp.exp2(products[rows, left] * (scale * LOG2E) + bias[rows, :])
            products[rows, left] = expon
            acc = acc + expon.reshape(CHUNK // 8, 8, BLOCK).sum(0)
        inverse = 1.0 / jnp.sum(acc, axis=0, keepdims=True)
        acc = jnp.zeros((8, BLOCK), F32)
        for start in range(0, cand, CHUNK):
            rows = slice(start, start + CHUNK)
            term = (products[rows, left] * inverse) * products[rows, right]
            acc = acc + term.reshape(CHUNK // 8, 8, BLOCK).sum(0)
        mean = jnp.sum(acc, axis=0, keepdims=True)
        for start in range(0, cand, CHUNK):
            rows = slice(start, start + CHUNK)
            prob = products[rows, left] * inverse
            weights[rows, left] = (prob * (products[rows, right] - mean)).astype(BF16)
            weights[rows, right] = prob.astype(BF16)

    def gather_rows(b, g, hh, weights):
        first = pl.multiple_of(b * BLOCK, BLOCK)
        top = C * g + 64 * hh
        pair = jnp.concatenate(
            [kvt[top : top + 64, pl.ds(first, WINDOW)], kvt[top : top + 64, ext:]], axis=1
        )
        result = nn(pair, weights[:, C * hh : C * hh + C])
        da[top : top + 32, pl.ds(first, BLOCK)] = result[:32, :BLOCK] * scale
        da[top + 32 : top + 64, pl.ds(first, BLOCK)] = result[32:, BLOCK:]

    def spread(b, g, weights):
        first = pl.multiple_of(b * BLOCK, BLOCK)
        cols = slice(C * g, C * g + C)
        stack = jnp.concatenate([operands(b, g, hh) for hh in range(4)], axis=0)
        total = nn(weights[...], stack)
        dkv[pl.ds(first, WINDOW), cols] += total[:WINDOW]
        dkv[ext:, cols] += total[WINDOW:]

    def step(b, carry):
        near = neighbors[:, pl.ds(pl.multiple_of(head * own + b * BLOCK, BLOCK), BLOCK)]
        shifted = (near - (head * own + b * BLOCK - SIDE)) & (rows_all - 1)
        index = jnp.where(near < rows_all, shifted, near - rows_all + WINDOW)
        for start in range(0, cand, CHUNK):
            rows = lax.broadcasted_iota(jnp.int32, (CHUNK, BLOCK), 0) + start
            count = jnp.zeros((CHUNK, BLOCK), F32)
            for slot in range(NBR):
                count = count + jnp.where(rows == index[slot : slot + 1, :], 1.0, 0.0)
            bias[start : start + CHUNK, :] = jnp.where(count > 0.5, jnp.log(count) * LOG2E, -1e30)
        before = jnp.maximum(b - 1, 0)
        after = jnp.minimum(b + 1, last)
        for hh in range(4):
            multiply(b, 1, hh, products1)
            weigh(hh, products0, weights0)
            gather_rows(before, 1, hh, weights1)
        spread(before, 1, weights1)
        for hh in range(4):
            multiply(after, 0, hh, products0)
            weigh(hh, products1, weights1)
            gather_rows(b, 0, hh, weights0)
        spread(b, 0, weights0)
        return carry

    weights1[...] = jnp.zeros_like(weights1)
    for hh in range(4):
        multiply(0, 0, hh, products0)
    lax.fori_loop(0, own // BLOCK, step, 0)
    for hh in range(4):
        gather_rows(last, 1, hh, weights1)
    spread(last, 1, weights1)
    col_scale = jnp.where((lax.broadcasted_iota(jnp.int32, (128, 2 * C), 1) & 63) < 32, scale, 1.0)
    for start in range(0, full, 128):
        rows = slice(start, start + 128)
        dkvt[:, rows] = (dkv[rows, :] * col_scale).astype(BF16).T
    own_grads = pltpu.roll(da[...], SIDE, 1).astype(BF16)
    summed[:, :ext] = (tn(wkv[...], dkvt[:, :ext]) + tn(wq[...], own_grads)).astype(BF16)
    summed[:, ext:] = tn(wkv[...], dkvt[:, ext:]).astype(BF16)
    grads[0] = nt(own_grads, xe[:, :ext]).astype(BF16)
    grads[1] = nt(dkvt[...], xe[...]).astype(BF16)
    grads[2] = nt(da[:, :own].astype(BF16), dy[...]).astype(BF16)
    for step_out, out in enumerate((o0, o1, o2, o3)):
        target = (head + step_out) & 3
        out[...] = summed[pl.ds(pl.multiple_of(target * 64, 64), 64), :]
    for target in range(4):
        for k in range(2):
            top = 128 * target + 64 * k
            for kind, (which, low) in enumerate(((0, 0), (1, 0), (1, 32), (2, 32))):
                sums[target, 64 * kind + 32 * k : 64 * kind + 32 * k + 32, :] = grads[
                    which, top + low : top + low + 32, :
                ]


def add_up(r0, r1, r2, r3, b0, b1, b2):
    border = b0.shape[1]
    first = r0.shape[1] - 3 * border
    for peer, out in enumerate((b0, b1, b2)):
        cols = slice(first + peer * border, first + (peer + 1) * border)
        out[...] = sum(part[:, cols].astype(F32) for part in (r0, r1, r2, r3)).astype(BF16)


def finish(place, r0, r1, r2, r3, b0, b1, b2, grad_in, lists, out, padded):
    head = place[0]
    rows = grad_in.shape[1]
    own = rows // 4
    ext = own + 2 * SIDE
    padded[...] = jnp.zeros_like(padded)
    for step, part in enumerate((r0, r1, r2, r3)):
        source = (head - step + 4) & 3
        first = pl.multiple_of(source * own, own)
        padded[:, pl.ds(first, ext)] += part[:, :ext].astype(F32)
    padded[:, : 2 * SIDE] += padded[:, rows:]
    aligned = pltpu.roll(padded[:, :rows], rows - SIDE, 1)
    back = jnp.concatenate([b0[...], b1[...], b2[...]], axis=1)
    for start in range(0, rows, 512):
        cols = slice(start, start + 512)
        returned = nt(back, one_hot_rows(lists[...], start, 512))
        out[:, cols] = grad_in[:, cols].astype(F32) + aligned[:, cols] + returned


def kernel_call(body, out_shape, inputs, scratch=(), mib=48, loose=()):
    specs = []
    for place, value in enumerate(inputs):
        if value.dtype == jnp.int32 and value.size == 1:
            specs.append(pl.BlockSpec(memory_space=pltpu.SMEM))
        elif place in loose:
            specs.append(pl.BlockSpec(memory_space=pltpu.HBM))
        else:
            specs.append(vmem_spec())
    outs = [vmem_spec() for _ in out_shape] if isinstance(out_shape, (list, tuple)) else vmem_spec()
    return pl.pallas_call(
        body,
        out_shape=out_shape,
        in_specs=specs,
        out_specs=outs,
        scratch_shapes=list(scratch),
        compiler_params=pltpu.CompilerParams(vmem_limit_bytes=mib * 1024 * 1024),
    )(*inputs)


def sds(shape, dtype):
    return jax.ShapeDtypeStruct(shape, dtype)


def attend_call(place, *args):
    *inputs, own, ext, full, cand = args
    return kernel_call(
        attend,
        [sds((64, full), BF16)] * 4 + [sds((4, C, C), BF16)],
        (place, *inputs),
        [
            pltpu.VMEM((C, full), BF16),
            pltpu.VMEM((C, own), BF16),
            pltpu.VMEM((2 * C, C), BF16),
            pltpu.VMEM((2 * C, C), BF16),
            pltpu.VMEM((2 * C, C), BF16),
            pltpu.VMEM((ext, 2 * C), BF16),
            pltpu.VMEM((own, 2 * C), BF16),
            pltpu.VMEM((2 * C, full), BF16),
            pltpu.VMEM((full, 2 * C), BF16),
            pltpu.VMEM((full, 2 * C), F32),
            pltpu.VMEM((2 * C, ext), F32),
            pltpu.VMEM((2 * C, full), BF16),
            pltpu.VMEM((3, 2 * C, C), BF16),
            pltpu.VMEM((C, full), BF16),
            pltpu.VMEM((cand, BLOCK), F32),
            pltpu.VMEM((cand, 4 * C), F32),
            pltpu.VMEM((cand, 4 * C), F32),
            pltpu.VMEM((cand, 4 * C), BF16),
            pltpu.VMEM((cand, 4 * C), BF16),
        ],
    )


def local(tokens, grad_in, w_qkv, w_out, neighbors, send_rows):
    groups = lax.axis_size("tile")
    border = send_rows.shape[2]
    offsets = (1, groups - 1, groups // 2)
    rows = tokens.shape[1]
    own = rows // 4
    ext = own + 2 * SIDE
    full = ext + 3 * border
    cand = WINDOW + 3 * border
    place = lax.axis_index("head").reshape(1).astype(jnp.int32)
    lists = send_rows.reshape(1, 3 * border)
    width = ext + own + 4 * C

    with jax.named_scope("border_rows"):
        halo = kernel_call(
            choose,
            sds((64, 3 * border), BF16),
            (tokens, lists),
            [pltpu.VMEM((64, rows), BF16), pltpu.SemaphoreType.DMA((4,))],
            loose=(0,),
        )
    with jax.named_scope("prepare"):
        chunks = kernel_call(
            prepare,
            [sds((64, width), BF16)] * 4,
            (place, tokens, grad_in, w_qkv, w_out, halo),
            [
                pltpu.VMEM((64, rows), BF16),
                pltpu.VMEM((3, 64, C), BF16),
                pltpu.VMEM((64, C), BF16),
                pltpu.VMEM((64, rows + 2 * SIDE), BF16),
                pltpu.SemaphoreType.DMA((7,)),
            ],
            loose=(1, 2, 3, 4),
        )
    with jax.named_scope("border_rows"):
        mine = jnp.concatenate(
            [
                passed_along(halo[:, peer * border : (peer + 1) * border], "tile", offsets[peer])
                for peer in range(3)
            ],
            axis=1,
        )
        spread = lax.all_to_all(
            jnp.broadcast_to(mine[None], (4, 64, 3 * border)), "head", 0, 0
        )
    with jax.named_scope("exchange"):
        chunks = [chunks[0]] + [passed_along(chunks[step], "head", step) for step in (1, 2, 3)]
    with jax.named_scope("attention"):
        *parts, sums = attend_call(place, *chunks, spread, neighbors, own, ext, full, cand)
    with jax.named_scope("return"):
        parts = [parts[0]] + [passed_along(parts[step], "head", step) for step in (1, 2, 3)]
    with jax.named_scope("weight_sums"):
        value = lax.all_to_all(
            sums.reshape(32, C // 8, C), ("tile", "head"), 0, 0, axis_index_groups=plates(4)
        )
        value = value.astype(F32).sum(0).astype(BF16)
        *parts, value = lax.optimization_barrier((*parts, value))
    with jax.named_scope("return"):
        back = kernel_call(add_up, [sds((64, border), BF16)] * 3, tuple(parts))
        back = [
            passed_along(back[peer], "tile", (groups - offsets[peer]) % groups)
            for peer in range(3)
        ]
    with jax.named_scope("weight_sums"):
        line = [[16 * y + 2 * z + c for z in range(8)] for y in range(4) for c in range(2)]
        piece = (8, C // 8, C)
        value = grouped(jnp.broadcast_to(value[None], piece), line)
        value = value.astype(F32).sum(0)
        *back, value = lax.optimization_barrier((*back, value))
        value = grouped(jnp.broadcast_to(value[None], piece), plates(1))
        grad_scale = 1.0 / math.sqrt(rows * groups)
        value = value.reshape(4, 64, C) * grad_scale
    with jax.named_scope("return"):
        d_tokens = kernel_call(
            finish,
            sds((64, rows), F32),
            (place, *parts, *back, grad_in, lists),
            [pltpu.VMEM((64, rows + 2 * SIDE), F32)],
        )
    return (d_tokens, value[:3], value[3])


def solution(mesh):
    return jax.shard_map(
        local,
        mesh=mesh,
        in_specs=(
            P("head", "tile"),
            P("head", "tile"),
            P(None, "head", None),
            P("head", None),
            P(None, "tile"),
            P("tile", None, None),
        ),
        out_specs=(P("head", "tile"), P(None, "head", None), P("head", None)),
        check_vma=False,
    )
```

```python
import math

import jax
import jax.numpy as jnp
from jax import lax
from jax.experimental import pallas as pl
from jax.experimental.pallas import tpu as pltpu
from jax.sharding import PartitionSpec as P

C = 256
HEADS = 8
NBR = 9
HEAD_DIM = 32
BLOCK = 128
SIDE = 64
CHUNK = 128
PARTS = 32
WINDOW = BLOCK + 2 * SIDE
LOG2E = math.log2(math.e)
F32 = jnp.float32
BF16 = jnp.bfloat16


def passed_along(value, axis, steps):
    count = lax.axis_size(axis)
    pairs = [(source, (source + steps) % count) for source in range(count)]
    return lax.ppermute(value, axis, pairs)


def rank(y, z, core):
    return 16 * y + 2 * z + core


PLATES = [[rank(y, z, core) for y in range(4) for core in range(2)] for z in range(8)]
SHEETS = [
    [rank(y, z, core) * 4 + head for z in range(8) for head in range(4)]
    for y in range(4)
    for core in range(2)
]


def vmem_spec():
    return pl.BlockSpec(memory_space=pltpu.VMEM)


def nt(a, b):
    return lax.dot_general(a, b, (((1,), (1,)), ((), ())), preferred_element_type=F32)


def tn(a, b):
    return lax.dot_general(a, b, (((0,), (0,)), ((), ())), preferred_element_type=F32)


def nn(a, b):
    return jnp.dot(a, b, preferred_element_type=F32)


def one_hot_rows(lists, start, count):
    rows = lax.broadcasted_iota(jnp.int32, (count, lists.shape[1]), 0) + start
    return jnp.where(rows == lists, 1.0, 0.0).astype(BF16)


def choose(tokens, lists, halo, x, sems):
    rows = tokens.shape[1]
    quarter = rows // 4
    fetches = [
        pltpu.make_async_copy(
            tokens.at[:, pl.ds(part * quarter, quarter)],
            x.at[:, pl.ds(part * quarter, quarter)],
            sems.at[part],
        )
        for part in range(4)
    ]
    for fetch in fetches:
        fetch.start()
    chosen = jnp.zeros(halo.shape, F32)
    for part, fetch in enumerate(fetches):
        fetch.wait()
        for start in range(part * quarter, (part + 1) * quarter, 512):
            chosen = chosen + nn(x[:, start : start + 512], one_hot_rows(lists[...], start, 512))
    halo[...] = chosen.astype(BF16)


def prepare(
    place, tokens, grad_in, w_qkv, w_out, halo, out0, out1, out2, out3, x, wv, wo, padded, sems
):
    head = place[0]
    rows = tokens.shape[1]
    own = rows // 4
    ext = own + 2 * SIDE
    base = ext + own
    outs = (out0, out1, out2, out3)
    fetch_x = pltpu.make_async_copy(tokens, x, sems.at[0])
    fetch_v = pltpu.make_async_copy(w_qkv, wv, sems.at[1])
    fetch_o = pltpu.make_async_copy(w_out, wo, sems.at[2])
    fetches = [
        pltpu.make_async_copy(
            grad_in.at[:, pl.ds(pl.multiple_of(((head + step) & 3) * own, own), own)],
            out.at[:, pl.ds(ext, own)],
            sems.at[3 + step],
        )
        for step, out in enumerate(outs)
    ]
    fetch_x.start()
    fetch_v.start()
    fetch_o.start()
    for fetch in fetches:
        fetch.start()
    fetch_x.wait()
    shifted = pltpu.roll(x[...].astype(F32), SIDE, 1).astype(BF16)
    padded[:, :rows] = shifted
    padded[:, rows:] = shifted[:, : 2 * SIDE]
    for step, out in enumerate(outs):
        first = pl.multiple_of(((head + step) & 3) * own, own)
        out[:, :ext] = padded[:, pl.ds(first, ext)]
    fetch_v.wait()
    fetch_o.wait()
    for out in outs:
        for kind in range(3):
            out[:, base + kind * C : base + (kind + 1) * C] = wv[kind]
        out[:, base + 3 * C :] = wo[...]
    for fetch in fetches:
        fetch.wait()


def masks(place, neighbors, bias):
    head = place[0]
    rows_all = neighbors.shape[1]
    blocks, cand, _ = bias.shape

    def step(b, carry):
        first = head * (rows_all // 4) + b * BLOCK
        near = neighbors[:, pl.ds(pl.multiple_of(first, BLOCK), BLOCK)]
        shifted = (near - (first - SIDE)) & (rows_all - 1)
        index = jnp.where(near < rows_all, shifted, near - rows_all + WINDOW)
        for start in range(0, cand, CHUNK):
            rows = lax.broadcasted_iota(jnp.int32, (CHUNK, BLOCK), 0) + start
            count = jnp.zeros((CHUNK, BLOCK), F32)
            for slot in range(NBR):
                count = count + jnp.where(rows == index[slot : slot + 1, :], 1.0, 0.0)
            bias[b, start : start + CHUNK, :] = jnp.where(
                count > 0.5, jnp.log(count) * LOG2E, -1e30
            )
        return carry

    lax.fori_loop(0, blocks, step, 0)


def attend(
    place, c0, c1, c2, c3, far, bias, o0, o1, o2, o3, sums,
    xe, dy, wq, wkv, wo, qs, ds, kvt, kv, dkv, da, dkvt, grads, summed,
    products0, products1, weights0, weights1, means0, means1, qt, dt,
):
    head = place[0]
    own = dy.shape[1]
    ext = own + 2 * SIDE
    full = xe.shape[1]
    border = full - ext
    cand = WINDOW + border
    scale = 1.0 / math.sqrt(HEAD_DIM)
    wq[...] = jnp.zeros_like(wq)
    wo[...] = jnp.zeros_like(wo)
    xe[:, ext:] = far[...].reshape(C, border)
    for step, chunk in enumerate((c0, c1, c2, c3)):
        source = (head - step + 4) & 3
        row = pl.multiple_of(source * 64, 64)
        xe[pl.ds(row, 64), :ext] = chunk[:, :ext]
        dy[pl.ds(row, 64), :] = chunk[:, ext : ext + own]
        base = ext + own
        for k in range(2):
            dest = pl.multiple_of(source * 128 + 64 * k, 64)
            part = slice(32 * k, 32 * k + 32)
            wq[pl.ds(dest, 32), :] = chunk[part, base : base + C]
            wkv[pl.ds(dest, 32), :] = chunk[part, base + C : base + 2 * C]
            wkv[pl.ds(dest + 32, 32), :] = chunk[part, base + 2 * C : base + 3 * C]
            wo[pl.ds(dest + 32, 32), :] = chunk[part, base + 3 * C :]
    for start in range(0, full, 256):
        cols = slice(start, start + 256)
        block = nn(wkv[...], xe[:, cols]).astype(BF16)
        kvt[:, cols] = block
        kv[cols, :] = block.T
    for start in range(0, ext, 384):
        cols = slice(start, start + 384)
        qs[cols, :] = nn(wq[...], xe[:, cols]).astype(BF16).T
    for start in range(0, own, 256):
        cols = slice(start, start + 256)
        block = nn(wo[...], dy[:, cols]).astype(BF16)
        dt[:, cols] = block
        ds[cols, :] = block.T
        qt[:, cols] = qs[start + SIDE : start + SIDE + 256, :].T
    dkv[...] = jnp.zeros_like(dkv)
    da[:, own:] = jnp.zeros((2 * C, 2 * SIDE), F32)
    lane_head = lax.broadcasted_iota(jnp.int32, (BLOCK, C), 1) // 64

    zero = jnp.zeros((BLOCK, C), BF16)
    last = own // BLOCK - 1

    def operands(b, g, hh):
        first = pl.multiple_of(b * BLOCK, BLOCK)
        cols = slice(C * g, C * g + C)
        mine = lane_head == hh
        query = jnp.where(mine, qs[pl.ds(first + SIDE, BLOCK), cols], zero)
        dout = jnp.where(mine, ds[pl.ds(first, BLOCK), cols], zero)
        return jnp.concatenate([query, dout], axis=0)

    def multiply(b, g, hh, products):
        first = pl.multiple_of(b * BLOCK, BLOCK)
        cols = slice(C * g, C * g + C)
        out = slice(C * hh, C * hh + 2 * C)
        stack = jnp.concatenate([operands(b, g, hh), operands(b, g, hh + 1)], axis=0)
        products[:WINDOW, out] = nt(kv[pl.ds(first, WINDOW), cols], stack)
        products[WINDOW:, out] = nt(kv[ext:, cols], stack)

    def first_pass(block, hh, products):
        left = slice(C * hh, C * hh + BLOCK)
        acc = jnp.zeros((PARTS, BLOCK), F32)
        for start in range(0, cand, CHUNK):
            rows = slice(start, start + CHUNK)
            expon = jnp.exp2(products[rows, left] * (scale * LOG2E) + bias[block, rows, :])
            products[rows, left] = expon
            acc = acc + expon.reshape(CHUNK // PARTS, PARTS, BLOCK).sum(0)
        return 1.0 / jnp.sum(acc, axis=0, keepdims=True)

    def second_pass(hh, products, weights, means, inverse):
        left = slice(C * hh, C * hh + BLOCK)
        right = slice(C * hh + BLOCK, C * hh + C)
        acc = jnp.zeros((PARTS, BLOCK), F32)
        for start in range(0, cand, CHUNK):
            rows = slice(start, start + CHUNK)
            prob = products[rows, left] * inverse
            term = prob * products[rows, right]
            weights[rows, left] = term.astype(BF16)
            weights[rows, right] = prob.astype(BF16)
            acc = acc + term.reshape(CHUNK // PARTS, PARTS, BLOCK).sum(0)
        means[hh : hh + 1, :] = jnp.sum(acc, axis=0, keepdims=True)

    def gather_rows(b, g, hh, weights, means):
        first = pl.multiple_of(b * BLOCK, BLOCK)
        top = C * g + 64 * hh
        pair = jnp.concatenate(
            [kvt[top : top + 64, pl.ds(first, WINDOW)], kvt[top : top + 64, ext:]], axis=1
        )
        result = nn(pair, weights[:, C * hh : C * hh + C])
        grad_query = result[:32, :BLOCK] - result[:32, BLOCK:] * means[hh : hh + 1, :]
        da[top : top + 32, pl.ds(first, BLOCK)] = grad_query * scale
        da[top + 32 : top + 64, pl.ds(first, BLOCK)] = result[32:, BLOCK:]

    def spread(b, g, hh, weights, means):
        first = pl.multiple_of(b * BLOCK, BLOCK)
        top = C * g + 64 * hh
        query = qt[top : top + 64, pl.ds(first, BLOCK)]
        dout = dt[top : top + 64, pl.ds(first, BLOCK)]
        second = dout - (query.astype(F32) * means[hh : hh + 1, :]).astype(BF16)
        both = jnp.concatenate([query, second], axis=1)
        cols = slice(C * hh, C * hh + C)
        dkv[top : top + 64, pl.ds(first, WINDOW)] += nt(both, weights[:WINDOW, cols])
        dkv[top : top + 64, ext:] += nt(both, weights[WINDOW:, cols])

    def phase(block, ahead, group, behind, products, weights, means, products_next, weights_done, means_done):
        inv0 = first_pass(block, 0, products)
        multiply(*ahead, 0, products_next)
        second_pass(0, products, weights, means, inv0)
        gather_rows(*behind, 0, weights_done, means_done)
        spread(*behind, 0, weights_done, means_done)
        inv1 = first_pass(block, 1, products)
        second_pass(1, products, weights, means, inv1)
        gather_rows(*behind, 1, weights_done, means_done)
        spread(*behind, 1, weights_done, means_done)
        inv2 = first_pass(block, 2, products)
        multiply(*ahead, 2, products_next)
        second_pass(2, products, weights, means, inv2)
        gather_rows(*behind, 2, weights_done, means_done)
        spread(*behind, 2, weights_done, means_done)
        inv3 = first_pass(block, 3, products)
        second_pass(3, products, weights, means, inv3)
        gather_rows(*behind, 3, weights_done, means_done)
        spread(*behind, 3, weights_done, means_done)

    def step(b, carry):
        before = jnp.maximum(b - 1, 0)
        after = jnp.minimum(b + 1, last)
        phase(b, (b, 1), 0, (before, 1), products0, weights0, means0, products1, weights1, means1)
        phase(b, (after, 0), 1, (b, 0), products1, weights1, means1, products0, weights0, means0)
        return carry

    weights1[...] = jnp.zeros_like(weights1)
    means0[...] = jnp.zeros_like(means0)
    means1[...] = jnp.zeros_like(means1)
    for hh in (0, 2):
        multiply(0, 0, hh, products0)
    lax.fori_loop(0, own // BLOCK, step, 0)
    for hh in range(4):
        gather_rows(last, 1, hh, weights1, means1)
        spread(last, 1, hh, weights1, means1)
    row_scale = jnp.where((lax.broadcasted_iota(jnp.int32, (2 * C, 128), 0) & 63) < 32, scale, 1.0)
    for start in range(0, full, 128):
        cols = slice(start, start + 128)
        dkvt[:, cols] = (dkv[:, cols] * row_scale).astype(BF16)
    own_grads = pltpu.roll(da[...], SIDE, 1).astype(BF16)
    summed[:, :ext] = (tn(wkv[...], dkvt[:, :ext]) + tn(wq[...], own_grads)).astype(BF16)
    summed[:, ext:] = tn(wkv[...], dkvt[:, ext:]).astype(BF16)
    grads[0] = nt(own_grads, xe[:, :ext]).astype(BF16)
    grads[1] = nt(dkvt[...], xe[...]).astype(BF16)
    grads[2] = nt(da[:, :own].astype(BF16), dy[...]).astype(BF16)
    for step_out, out in enumerate((o0, o1, o2, o3)):
        target = (head + step_out) & 3
        out[...] = summed[pl.ds(pl.multiple_of(target * 64, 64), 64), :]
    for target in range(4):
        for k in range(2):
            top = 128 * target + 64 * k
            for kind, (which, low) in enumerate(((0, 0), (1, 0), (1, 32), (2, 32))):
                sums[2 * kind + k, target] = grads[which, top + low : top + low + 32, :]


def add_up(r0, r1, r2, r3, b0, b1, b2):
    border = b0.shape[1]
    first = r0.shape[1] - 3 * border
    for peer, out in enumerate((b0, b1, b2)):
        cols = slice(first + peer * border, first + (peer + 1) * border)
        out[...] = sum(part[:, cols].astype(F32) for part in (r0, r1, r2, r3)).astype(BF16)


def finish(place, r0, r1, r2, r3, b0, b1, b2, grad_in, lists, out, padded):
    head = place[0]
    rows = grad_in.shape[1]
    own = rows // 4
    ext = own + 2 * SIDE
    padded[...] = jnp.zeros_like(padded)
    for step, part in enumerate((r0, r1, r2, r3)):
        source = (head - step + 4) & 3
        first = pl.multiple_of(source * own, own)
        padded[:, pl.ds(first, ext)] += part[:, :ext].astype(F32)
    padded[:, : 2 * SIDE] += padded[:, rows:]
    aligned = pltpu.roll(padded[:, :rows], rows - SIDE, 1)
    back = jnp.concatenate([b0[...], b1[...], b2[...]], axis=1)
    for start in range(0, rows, 512):
        cols = slice(start, start + 512)
        returned = nt(back, one_hot_rows(lists[...], start, 512))
        out[:, cols] = grad_in[:, cols].astype(F32) + aligned[:, cols] + returned


def kernel_call(body, out_shape, inputs, scratch=(), mib=12, loose=()):
    specs = []
    for place, value in enumerate(inputs):
        if value.dtype == jnp.int32 and value.size == 1:
            specs.append(pl.BlockSpec(memory_space=pltpu.SMEM))
        elif place in loose:
            specs.append(pl.BlockSpec(memory_space=pltpu.HBM))
        else:
            specs.append(vmem_spec())
    outs = [vmem_spec() for _ in out_shape] if isinstance(out_shape, (list, tuple)) else vmem_spec()
    return pl.pallas_call(
        body,
        out_shape=out_shape,
        in_specs=specs,
        out_specs=outs,
        scratch_shapes=list(scratch),
        compiler_params=pltpu.CompilerParams(vmem_limit_bytes=mib * 1024 * 1024),
    )(*inputs)


def sds(shape, dtype):
    return jax.ShapeDtypeStruct(shape, dtype)


def attend_call(place, *args):
    *inputs, neighbors, own, ext, full, cand = args
    with jax.named_scope("masks"):
        bias = kernel_call(masks, sds((own // BLOCK, cand, BLOCK), F32), (place, neighbors))
    return kernel_call(
        attend,
        [sds((64, full), BF16)] * 4 + [sds((8, 4, C // 8, C), BF16)],
        (place, *inputs, bias),
        [
            pltpu.VMEM((C, full), BF16),
            pltpu.VMEM((C, own), BF16),
            pltpu.VMEM((2 * C, C), BF16),
            pltpu.VMEM((2 * C, C), BF16),
            pltpu.VMEM((2 * C, C), BF16),
            pltpu.VMEM((ext, 2 * C), BF16),
            pltpu.VMEM((own, 2 * C), BF16),
            pltpu.VMEM((2 * C, full), BF16),
            pltpu.VMEM((full, 2 * C), BF16),
            pltpu.VMEM((2 * C, full), F32),
            pltpu.VMEM((2 * C, ext), F32),
            pltpu.VMEM((2 * C, full), BF16),
            pltpu.VMEM((3, 2 * C, C), BF16),
            pltpu.VMEM((C, full), BF16),
            pltpu.VMEM((cand, 4 * C), F32),
            pltpu.VMEM((cand, 4 * C), F32),
            pltpu.VMEM((cand, 4 * C), BF16),
            pltpu.VMEM((cand, 4 * C), BF16),
            pltpu.VMEM((8, BLOCK), F32),
            pltpu.VMEM((8, BLOCK), F32),
            pltpu.VMEM((2 * C, own), BF16),
            pltpu.VMEM((2 * C, own), BF16),
        ],
        mib=36,
    )


def local(tokens, grad_in, w_qkv, w_out, neighbors, send_rows):
    groups = lax.axis_size("tile")
    border = send_rows.shape[2]
    offsets = (1, groups - 1, groups // 2)
    rows = tokens.shape[1]
    own = rows // 4
    ext = own + 2 * SIDE
    full = ext + 3 * border
    cand = WINDOW + 3 * border
    place = lax.axis_index("head").reshape(1).astype(jnp.int32)
    lists = send_rows.reshape(1, 3 * border)
    width = ext + own + 4 * C

    with jax.named_scope("border_rows"):
        halo = kernel_call(
            choose,
            sds((64, 3 * border), BF16),
            (tokens, lists),
            [pltpu.VMEM((64, rows), BF16), pltpu.SemaphoreType.DMA((4,))],
            loose=(0,),
        )
    with jax.named_scope("prepare"):
        chunks = kernel_call(
            prepare,
            [sds((64, width), BF16)] * 4,
            (place, tokens, grad_in, w_qkv, w_out, halo),
            [
                pltpu.VMEM((64, rows), BF16),
                pltpu.VMEM((3, 64, C), BF16),
                pltpu.VMEM((64, C), BF16),
                pltpu.VMEM((64, rows + 2 * SIDE), BF16),
                pltpu.SemaphoreType.DMA((7,)),
            ],
            loose=(1, 2, 3, 4),
        )
    with jax.named_scope("border_rows"):
        mine = jnp.concatenate(
            [
                passed_along(halo[:, peer * border : (peer + 1) * border], "tile", offsets[peer])
                for peer in range(3)
            ],
            axis=1,
        )
        spread = lax.all_to_all(
            jnp.broadcast_to(mine[None], (4, 64, 3 * border)), "head", 0, 0
        )
    with jax.named_scope("exchange"):
        chunks = [chunks[0]] + [passed_along(chunks[step], "head", step) for step in (1, 2, 3)]
    with jax.named_scope("attention"):
        *parts, sums = attend_call(place, *chunks, spread, neighbors, own, ext, full, cand)
    with jax.named_scope("return"):
        parts = [parts[0]] + [passed_along(parts[step], "head", step) for step in (1, 2, 3)]
    with jax.named_scope("weight_sums"):
        value = lax.all_to_all(sums, "tile", 0, 0, axis_index_groups=PLATES)
        value = value.astype(F32).sum(0).astype(BF16)
        *parts, value = lax.optimization_barrier((*parts, value))
    with jax.named_scope("return"):
        back = kernel_call(add_up, [sds((64, border), BF16)] * 3, tuple(parts))
        back = [
            passed_along(back[peer], "tile", (groups - offsets[peer]) % groups)
            for peer in range(3)
        ]
    with jax.named_scope("weight_sums"):
        value = jnp.broadcast_to(value[None], (8, 4, C // 8, C)).reshape(32, C // 8, C)
        value = lax.all_to_all(value, ("tile", "head"), 0, 0, axis_index_groups=SHEETS)
        value = value.astype(F32).sum(0) * (1.0 / math.sqrt(rows * groups))
        *back, value = lax.optimization_barrier((*back, value))
        value = jnp.broadcast_to(value[None], (8, C // 8, C))
        value = lax.all_to_all(value, "tile", 0, 0, axis_index_groups=PLATES)
        value = value.reshape(4, 64, C)
    with jax.named_scope("return"):
        d_tokens = kernel_call(
            finish,
            sds((64, rows), F32),
            (place, *parts, *back, grad_in, lists),
            [pltpu.VMEM((64, rows + 2 * SIDE), F32)],
        )
    return (d_tokens, value[:3], value[3])


def solution(mesh):
    return jax.shard_map(
        local,
        mesh=mesh,
        in_specs=(
            P("head", "tile"),
            P("head", "tile"),
            P(None, "head", None),
            P("head", None),
            P(None, "tile"),
            P("tile", None, None),
        ),
        out_specs=(P("head", "tile"), P(None, "head", None), P("head", None)),
        check_vma=False,
    )
```

```python
import math

import jax
import jax.numpy as jnp
from jax import lax
from jax.experimental import pallas as pl
from jax.experimental.pallas import tpu as pltpu
from jax.sharding import PartitionSpec as P

C = 256
HEADS = 8
NBR = 9
HEAD_DIM = 32
BLOCK = 128
SIDE = 64
CHUNK = 64
PARTS = 32
WINDOW = BLOCK + 2 * SIDE
LOG2E = math.log2(math.e)
F32 = jnp.float32
BF16 = jnp.bfloat16


def passed_along(value, axis, steps):
    count = lax.axis_size(axis)
    pairs = [(source, (source + steps) % count) for source in range(count)]
    return lax.ppermute(value, axis, pairs)


def grouped(value, groups):
    return lax.all_to_all(value, "tile", 0, 0, axis_index_groups=groups)


def plates(heads):
    return [
        [(16 * y + 2 * z + c) * heads + h for h in range(heads) for y in range(4) for c in range(2)]
        for z in range(8)
    ]


def vmem_spec():
    return pl.BlockSpec(memory_space=pltpu.VMEM)


def nt(a, b):
    return lax.dot_general(a, b, (((1,), (1,)), ((), ())), preferred_element_type=F32)


def tn(a, b):
    return lax.dot_general(a, b, (((0,), (0,)), ((), ())), preferred_element_type=F32)


def nn(a, b):
    return jnp.dot(a, b, preferred_element_type=F32)


def one_hot_rows(lists, start, count):
    rows = lax.broadcasted_iota(jnp.int32, (count, lists.shape[1]), 0) + start
    return jnp.where(rows == lists, 1.0, 0.0).astype(BF16)


def choose(tokens, lists, halo, x, sems):
    rows = tokens.shape[1]
    quarter = rows // 4
    fetches = [
        pltpu.make_async_copy(
            tokens.at[:, pl.ds(part * quarter, quarter)],
            x.at[:, pl.ds(part * quarter, quarter)],
            sems.at[part],
        )
        for part in range(4)
    ]
    for fetch in fetches:
        fetch.start()
    chosen = jnp.zeros(halo.shape, F32)
    for part, fetch in enumerate(fetches):
        fetch.wait()
        for start in range(part * quarter, (part + 1) * quarter, 512):
            chosen = chosen + nn(x[:, start : start + 512], one_hot_rows(lists[...], start, 512))
    halo[...] = chosen.astype(BF16)


def prepare(
    place, tokens, grad_in, w_qkv, w_out, halo, out0, out1, out2, out3, x, wv, wo, padded, sems
):
    head = place[0]
    rows = tokens.shape[1]
    own = rows // 4
    ext = own + 2 * SIDE
    base = ext + own
    outs = (out0, out1, out2, out3)
    fetch_x = pltpu.make_async_copy(tokens, x, sems.at[0])
    fetch_v = pltpu.make_async_copy(w_qkv, wv, sems.at[1])
    fetch_o = pltpu.make_async_copy(w_out, wo, sems.at[2])
    fetches = [
        pltpu.make_async_copy(
            grad_in.at[:, pl.ds(pl.multiple_of(((head + step) & 3) * own, own), own)],
            out.at[:, pl.ds(ext, own)],
            sems.at[3 + step],
        )
        for step, out in enumerate(outs)
    ]
    fetch_x.start()
    fetch_v.start()
    fetch_o.start()
    for fetch in fetches:
        fetch.start()
    fetch_x.wait()
    shifted = pltpu.roll(x[...].astype(F32), SIDE, 1).astype(BF16)
    padded[:, :rows] = shifted
    padded[:, rows:] = shifted[:, : 2 * SIDE]
    for step, out in enumerate(outs):
        first = pl.multiple_of(((head + step) & 3) * own, own)
        out[:, :ext] = padded[:, pl.ds(first, ext)]
    fetch_v.wait()
    fetch_o.wait()
    for out in outs:
        for kind in range(3):
            out[:, base + kind * C : base + (kind + 1) * C] = wv[kind]
        out[:, base + 3 * C :] = wo[...]
    for fetch in fetches:
        fetch.wait()


def attend(
    place, c0, c1, c2, c3, far, neighbors, o0, o1, o2, o3, sums,
    bias, xe, dy, wq, wkv, wo, qs, ds, kvt, kv, dkv, da, dkvt, grads, summed,
    products0, products1, weights0, weights1, means0, means1, qt, dt,
):
    head = place[0]
    own = dy.shape[1]
    ext = own + 2 * SIDE
    full = xe.shape[1]
    border = full - ext
    cand = WINDOW + border
    scale = 1.0 / math.sqrt(HEAD_DIM)
    wq[...] = jnp.zeros_like(wq)
    wo[...] = jnp.zeros_like(wo)
    xe[:, ext:] = far[...].reshape(C, border)
    for step, chunk in enumerate((c0, c1, c2, c3)):
        source = (head - step + 4) & 3
        row = pl.multiple_of(source * 64, 64)
        xe[pl.ds(row, 64), :ext] = chunk[:, :ext]
        dy[pl.ds(row, 64), :] = chunk[:, ext : ext + own]
        base = ext + own
        for k in range(2):
            dest = pl.multiple_of(source * 128 + 64 * k, 64)
            part = slice(32 * k, 32 * k + 32)
            wq[pl.ds(dest, 32), :] = chunk[part, base : base + C]
            wkv[pl.ds(dest, 32), :] = chunk[part, base + C : base + 2 * C]
            wkv[pl.ds(dest + 32, 32), :] = chunk[part, base + 2 * C : base + 3 * C]
            wo[pl.ds(dest + 32, 32), :] = chunk[part, base + 3 * C :]
    for start in range(0, full, 256):
        cols = slice(start, start + 256)
        block = nn(wkv[...], xe[:, cols]).astype(BF16)
        kvt[:, cols] = block
        kv[cols, :] = block.T
    for start in range(0, ext, 384):
        cols = slice(start, start + 384)
        qs[cols, :] = nn(wq[...], xe[:, cols]).astype(BF16).T
    for start in range(0, own, 256):
        cols = slice(start, start + 256)
        block = nn(wo[...], dy[:, cols]).astype(BF16)
        dt[:, cols] = block
        ds[cols, :] = block.T
        qt[:, cols] = qs[start + SIDE : start + SIDE + 256, :].T
    dkv[...] = jnp.zeros_like(dkv)
    da[:, own:] = jnp.zeros((2 * C, 2 * SIDE), F32)
    lane_head = lax.broadcasted_iota(jnp.int32, (BLOCK, C), 1) // 64

    zero = jnp.zeros((BLOCK, C), BF16)
    last = own // BLOCK - 1

    def operands(b, g, hh):
        first = pl.multiple_of(b * BLOCK, BLOCK)
        cols = slice(C * g, C * g + C)
        mine = lane_head == hh
        query = jnp.where(mine, qs[pl.ds(first + SIDE, BLOCK), cols], zero)
        dout = jnp.where(mine, ds[pl.ds(first, BLOCK), cols], zero)
        return jnp.concatenate([query, dout], axis=0)

    def multiply(b, g, hh, products):
        first = pl.multiple_of(b * BLOCK, BLOCK)
        cols = slice(C * g, C * g + C)
        out = slice(C * hh, C * hh + 2 * C)
        stack = jnp.concatenate([operands(b, g, hh), operands(b, g, hh + 1)], axis=0)
        products[:WINDOW, out] = nt(kv[pl.ds(first, WINDOW), cols], stack)
        products[WINDOW:, out] = nt(kv[ext:, cols], stack)

    def first_pass(block, hh, products):
        left = slice(C * hh, C * hh + BLOCK)
        acc = jnp.zeros((PARTS, BLOCK), F32)
        for start in range(0, cand, CHUNK):
            rows = slice(start, start + CHUNK)
            expon = jnp.exp2(products[rows, left] * (scale * LOG2E) + bias[rows, :])
            products[rows, left] = expon
            acc = acc + expon.reshape(CHUNK // PARTS, PARTS, BLOCK).sum(0)
        return 1.0 / jnp.sum(acc, axis=0, keepdims=True)

    def second_pass(hh, products, weights, means, inverse):
        left = slice(C * hh, C * hh + BLOCK)
        right = slice(C * hh + BLOCK, C * hh + C)
        acc = jnp.zeros((PARTS, BLOCK), F32)
        for start in range(0, cand, CHUNK):
            rows = slice(start, start + CHUNK)
            prob = products[rows, left] * inverse
            term = prob * products[rows, right]
            weights[rows, left] = term.astype(BF16)
            weights[rows, right] = prob.astype(BF16)
            acc = acc + term.reshape(CHUNK // PARTS, PARTS, BLOCK).sum(0)
        means[hh : hh + 1, :] = jnp.sum(acc, axis=0, keepdims=True)

    def gather_rows(b, g, hh, weights, means):
        first = pl.multiple_of(b * BLOCK, BLOCK)
        top = C * g + 64 * hh
        pair = jnp.concatenate(
            [kvt[top : top + 64, pl.ds(first, WINDOW)], kvt[top : top + 64, ext:]], axis=1
        )
        result = nn(pair, weights[:, C * hh : C * hh + C])
        grad_query = result[:32, :BLOCK] - result[:32, BLOCK:] * means[hh : hh + 1, :]
        da[top : top + 32, pl.ds(first, BLOCK)] = grad_query * scale
        da[top + 32 : top + 64, pl.ds(first, BLOCK)] = result[32:, BLOCK:]

    def spread(b, g, hh, weights, means):
        first = pl.multiple_of(b * BLOCK, BLOCK)
        top = C * g + 64 * hh
        query = qt[top : top + 64, pl.ds(first, BLOCK)]
        dout = dt[top : top + 64, pl.ds(first, BLOCK)]
        second = dout - (query.astype(F32) * means[hh : hh + 1, :]).astype(BF16)
        both = jnp.concatenate([query, second], axis=1)
        cols = slice(C * hh, C * hh + C)
        out = nt(both, weights[:, cols])
        dkv[top : top + 64, pl.ds(first, WINDOW)] += out[:, :WINDOW]
        dkv[top : top + 64, ext:] += out[:, WINDOW:]

    def phase(block, ahead, group, behind, products, weights, means, products_next, weights_done, means_done):
        inv0 = first_pass(block, 0, products)
        multiply(*ahead, 0, products_next)
        second_pass(0, products, weights, means, inv0)
        gather_rows(*behind, 0, weights_done, means_done)
        spread(*behind, 0, weights_done, means_done)
        inv1 = first_pass(block, 1, products)
        second_pass(1, products, weights, means, inv1)
        gather_rows(*behind, 1, weights_done, means_done)
        spread(*behind, 1, weights_done, means_done)
        inv2 = first_pass(block, 2, products)
        multiply(*ahead, 2, products_next)
        second_pass(2, products, weights, means, inv2)
        gather_rows(*behind, 2, weights_done, means_done)
        spread(*behind, 2, weights_done, means_done)
        inv3 = first_pass(block, 3, products)
        second_pass(3, products, weights, means, inv3)
        gather_rows(*behind, 3, weights_done, means_done)
        spread(*behind, 3, weights_done, means_done)

    def step(b, carry):
        near = neighbors[:, pl.ds(pl.multiple_of(head * own + b * BLOCK, BLOCK), BLOCK)]
        shifted = (near - (head * own + b * BLOCK - SIDE)) & (neighbors.shape[1] - 1)
        index = jnp.where(near < neighbors.shape[1], shifted, near - neighbors.shape[1] + WINDOW)
        for start in range(0, cand, CHUNK):
            rows = lax.broadcasted_iota(jnp.int32, (CHUNK, BLOCK), 0) + start
            count = jnp.zeros((CHUNK, BLOCK), F32)
            for slot in range(NBR):
                count = count + jnp.where(rows == index[slot : slot + 1, :], 1.0, 0.0)
            bias[start : start + CHUNK, :] = jnp.where(count > 0.5, jnp.log(count) * LOG2E, -1e30)
        before = jnp.maximum(b - 1, 0)
        after = jnp.minimum(b + 1, last)
        phase(b, (b, 1), 0, (before, 1), products0, weights0, means0, products1, weights1, means1)
        phase(b, (after, 0), 1, (b, 0), products1, weights1, means1, products0, weights0, means0)
        return carry

    weights1[...] = jnp.zeros_like(weights1)
    means0[...] = jnp.zeros_like(means0)
    means1[...] = jnp.zeros_like(means1)
    for hh in (0, 2):
        multiply(0, 0, hh, products0)
    lax.fori_loop(0, own // BLOCK, step, 0)
    for hh in range(4):
        gather_rows(last, 1, hh, weights1, means1)
        spread(last, 1, hh, weights1, means1)
    row_scale = jnp.where((lax.broadcasted_iota(jnp.int32, (2 * C, 128), 0) & 63) < 32, scale, 1.0)
    for start in range(0, full, 128):
        cols = slice(start, start + 128)
        dkvt[:, cols] = (dkv[:, cols] * row_scale).astype(BF16)
    own_grads = pltpu.roll(da[...], SIDE, 1).astype(BF16)
    summed[:, :ext] = (tn(wkv[...], dkvt[:, :ext]) + tn(wq[...], own_grads)).astype(BF16)
    summed[:, ext:] = tn(wkv[...], dkvt[:, ext:]).astype(BF16)
    grads[0] = nt(own_grads, xe[:, :ext]).astype(BF16)
    grads[1] = nt(dkvt[...], xe[...]).astype(BF16)
    grads[2] = nt(da[:, :own].astype(BF16), dy[...]).astype(BF16)
    for step_out, out in enumerate((o0, o1, o2, o3)):
        target = (head + step_out) & 3
        out[...] = summed[pl.ds(pl.multiple_of(target * 64, 64), 64), :]
    for target in range(4):
        for k in range(2):
            top = 128 * target + 64 * k
            for kind, (which, low) in enumerate(((0, 0), (1, 0), (1, 32), (2, 32))):
                sums[target, 64 * kind + 32 * k : 64 * kind + 32 * k + 32, :] = grads[
                    which, top + low : top + low + 32, :
                ]


def add_up(r0, r1, r2, r3, b0, b1, b2):
    border = b0.shape[1]
    first = r0.shape[1] - 3 * border
    for peer, out in enumerate((b0, b1, b2)):
        cols = slice(first + peer * border, first + (peer + 1) * border)
        out[...] = sum(part[:, cols].astype(F32) for part in (r0, r1, r2, r3)).astype(BF16)


def finish(place, r0, r1, r2, r3, b0, b1, b2, grad_in, lists, out, padded):
    head = place[0]
    rows = grad_in.shape[1]
    own = rows // 4
    ext = own + 2 * SIDE
    padded[...] = jnp.zeros_like(padded)
    for step, part in enumerate((r0, r1, r2, r3)):
        source = (head - step + 4) & 3
        first = pl.multiple_of(source * own, own)
        padded[:, pl.ds(first, ext)] += part[:, :ext].astype(F32)
    padded[:, : 2 * SIDE] += padded[:, rows:]
    aligned = pltpu.roll(padded[:, :rows], rows - SIDE, 1)
    back = jnp.concatenate([b0[...], b1[...], b2[...]], axis=1)
    for start in range(0, rows, 512):
        cols = slice(start, start + 512)
        returned = nt(back, one_hot_rows(lists[...], start, 512))
        out[:, cols] = grad_in[:, cols].astype(F32) + aligned[:, cols] + returned


def kernel_call(body, out_shape, inputs, scratch=(), mib=48, loose=()):
    specs = []
    for place, value in enumerate(inputs):
        if value.dtype == jnp.int32 and value.size == 1:
            specs.append(pl.BlockSpec(memory_space=pltpu.SMEM))
        elif place in loose:
            specs.append(pl.BlockSpec(memory_space=pltpu.HBM))
        else:
            specs.append(vmem_spec())
    outs = [vmem_spec() for _ in out_shape] if isinstance(out_shape, (list, tuple)) else vmem_spec()
    return pl.pallas_call(
        body,
        out_shape=out_shape,
        in_specs=specs,
        out_specs=outs,
        scratch_shapes=list(scratch),
        compiler_params=pltpu.CompilerParams(vmem_limit_bytes=mib * 1024 * 1024),
    )(*inputs)


def sds(shape, dtype):
    return jax.ShapeDtypeStruct(shape, dtype)


def attend_call(place, *args):
    *inputs, own, ext, full, cand = args
    return kernel_call(
        attend,
        [sds((64, full), BF16)] * 4 + [sds((4, C, C), BF16)],
        (place, *inputs),
        [
            pltpu.VMEM((cand, BLOCK), F32),
            pltpu.VMEM((C, full), BF16),
            pltpu.VMEM((C, own), BF16),
            pltpu.VMEM((2 * C, C), BF16),
            pltpu.VMEM((2 * C, C), BF16),
            pltpu.VMEM((2 * C, C), BF16),
            pltpu.VMEM((ext, 2 * C), BF16),
            pltpu.VMEM((own, 2 * C), BF16),
            pltpu.VMEM((2 * C, full), BF16),
            pltpu.VMEM((full, 2 * C), BF16),
            pltpu.VMEM((2 * C, full), F32),
            pltpu.VMEM((2 * C, ext), F32),
            pltpu.VMEM((2 * C, full), BF16),
            pltpu.VMEM((3, 2 * C, C), BF16),
            pltpu.VMEM((C, full), BF16),
            pltpu.VMEM((cand, 4 * C), F32),
            pltpu.VMEM((cand, 4 * C), F32),
            pltpu.VMEM((cand, 4 * C), BF16),
            pltpu.VMEM((cand, 4 * C), BF16),
            pltpu.VMEM((8, BLOCK), F32),
            pltpu.VMEM((8, BLOCK), F32),
            pltpu.VMEM((2 * C, own), BF16),
            pltpu.VMEM((2 * C, own), BF16),
        ],
    )


def local(tokens, grad_in, w_qkv, w_out, neighbors, send_rows):
    groups = lax.axis_size("tile")
    border = send_rows.shape[2]
    offsets = (1, groups - 1, groups // 2)
    rows = tokens.shape[1]
    own = rows // 4
    ext = own + 2 * SIDE
    full = ext + 3 * border
    cand = WINDOW + 3 * border
    place = lax.axis_index("head").reshape(1).astype(jnp.int32)
    lists = send_rows.reshape(1, 3 * border)
    width = ext + own + 4 * C

    with jax.named_scope("border_rows"):
        halo = kernel_call(
            choose,
            sds((64, 3 * border), BF16),
            (tokens, lists),
            [pltpu.VMEM((64, rows), BF16), pltpu.SemaphoreType.DMA((4,))],
            loose=(0,),
        )
    with jax.named_scope("prepare"):
        chunks = kernel_call(
            prepare,
            [sds((64, width), BF16)] * 4,
            (place, tokens, grad_in, w_qkv, w_out, halo),
            [
                pltpu.VMEM((64, rows), BF16),
                pltpu.VMEM((3, 64, C), BF16),
                pltpu.VMEM((64, C), BF16),
                pltpu.VMEM((64, rows + 2 * SIDE), BF16),
                pltpu.SemaphoreType.DMA((7,)),
            ],
            loose=(1, 2, 3, 4),
        )
    with jax.named_scope("border_rows"):
        mine = jnp.concatenate(
            [
                passed_along(halo[:, peer * border : (peer + 1) * border], "tile", offsets[peer])
                for peer in range(3)
            ],
            axis=1,
        )
        spread = lax.all_to_all(
            jnp.broadcast_to(mine[None], (4, 64, 3 * border)), "head", 0, 0
        )
    with jax.named_scope("exchange"):
        chunks = [chunks[0]] + [passed_along(chunks[step], "head", step) for step in (1, 2, 3)]
    with jax.named_scope("attention"):
        *parts, sums = attend_call(place, *chunks, spread, neighbors, own, ext, full, cand)
    with jax.named_scope("return"):
        parts = [parts[0]] + [passed_along(parts[step], "head", step) for step in (1, 2, 3)]
    with jax.named_scope("weight_sums"):
        value = lax.all_to_all(
            sums.reshape(32, C // 8, C), ("tile", "head"), 0, 0, axis_index_groups=plates(4)
        )
        value = value.astype(F32).sum(0).astype(BF16)
        *parts, value = lax.optimization_barrier((*parts, value))
    with jax.named_scope("return"):
        back = kernel_call(add_up, [sds((64, border), BF16)] * 3, tuple(parts))
        back = [
            passed_along(back[peer], "tile", (groups - offsets[peer]) % groups)
            for peer in range(3)
        ]
    with jax.named_scope("weight_sums"):
        line = [[16 * y + 2 * z + c for z in range(8)] for y in range(4) for c in range(2)]
        piece = (8, C // 8, C)
        value = grouped(jnp.broadcast_to(value[None], piece), line)
        grad_scale = 1.0 / math.sqrt(rows * groups)
        value = value.astype(F32).sum(0) * grad_scale
        *back, value = lax.optimization_barrier((*back, value))
        value = grouped(jnp.broadcast_to(value[None], piece), plates(1))
        value = value.reshape(4, 64, C)
    with jax.named_scope("return"):
        d_tokens = kernel_call(
            finish,
            sds((64, rows), F32),
            (place, *parts, *back, grad_in, lists),
            [pltpu.VMEM((64, rows + 2 * SIDE), F32)],
        )
    return (d_tokens, value[:3], value[3])


def solution(mesh):
    return jax.shard_map(
        local,
        mesh=mesh,
        in_specs=(
            P("head", "tile"),
            P("head", "tile"),
            P(None, "head", None),
            P("head", None),
            P(None, "tile"),
            P("tile", None, None),
        ),
        out_specs=(P("head", "tile"), P(None, "head", None), P("head", None)),
        check_vma=False,
    )
```

```python
import math

import jax
import jax.numpy as jnp
from jax import lax
from jax.experimental import pallas as pl
from jax.experimental.pallas import tpu as pltpu
from jax.sharding import PartitionSpec as P

C = 256
HEADS = 8
NBR = 9
HEAD_DIM = 32
BLOCK = 128
SIDE = 64
CHUNK = 64
PARTS = 32
WINDOW = BLOCK + 2 * SIDE
LOG2E = math.log2(math.e)
F32 = jnp.float32
BF16 = jnp.bfloat16


def passed_along(value, axis, steps):
    count = lax.axis_size(axis)
    pairs = [(source, (source + steps) % count) for source in range(count)]
    return lax.ppermute(value, axis, pairs)


def grouped(value, groups):
    return lax.all_to_all(value, "tile", 0, 0, axis_index_groups=groups)


def plates(heads):
    return [
        [(16 * y + 2 * z + c) * heads + h for h in range(heads) for y in range(4) for c in range(2)]
        for z in range(8)
    ]


def vmem_spec():
    return pl.BlockSpec(memory_space=pltpu.VMEM)


def nt(a, b):
    return lax.dot_general(a, b, (((1,), (1,)), ((), ())), preferred_element_type=F32)


def tn(a, b):
    return lax.dot_general(a, b, (((0,), (0,)), ((), ())), preferred_element_type=F32)


def nn(a, b):
    return jnp.dot(a, b, preferred_element_type=F32)


def one_hot_rows(lists, start, count):
    rows = lax.broadcasted_iota(jnp.int32, (count, lists.shape[1]), 0) + start
    return jnp.where(rows == lists, 1.0, 0.0).astype(BF16)


def choose(tokens, lists, halo, x, sems):
    rows = tokens.shape[1]
    quarter = rows // 4
    fetches = [
        pltpu.make_async_copy(
            tokens.at[:, pl.ds(part * quarter, quarter)],
            x.at[:, pl.ds(part * quarter, quarter)],
            sems.at[part],
        )
        for part in range(4)
    ]
    for fetch in fetches:
        fetch.start()
    chosen = jnp.zeros(halo.shape, F32)
    for part, fetch in enumerate(fetches):
        fetch.wait()
        for start in range(part * quarter, (part + 1) * quarter, 512):
            chosen = chosen + nn(x[:, start : start + 512], one_hot_rows(lists[...], start, 512))
    halo[...] = chosen.astype(BF16)


def prepare(
    place, tokens, grad_in, w_qkv, w_out, halo, out0, out1, out2, out3, x, wv, wo, padded, sems
):
    head = place[0]
    rows = tokens.shape[1]
    own = rows // 4
    ext = own + 2 * SIDE
    base = ext + own
    outs = (out0, out1, out2, out3)
    fetch_x = pltpu.make_async_copy(tokens, x, sems.at[0])
    fetch_v = pltpu.make_async_copy(w_qkv, wv, sems.at[1])
    fetch_o = pltpu.make_async_copy(w_out, wo, sems.at[2])
    fetches = [
        pltpu.make_async_copy(
            grad_in.at[:, pl.ds(pl.multiple_of(((head + step) & 3) * own, own), own)],
            out.at[:, pl.ds(ext, own)],
            sems.at[3 + step],
        )
        for step, out in enumerate(outs)
    ]
    fetch_x.start()
    fetch_v.start()
    fetch_o.start()
    for fetch in fetches:
        fetch.start()
    fetch_x.wait()
    shifted = pltpu.roll(x[...].astype(F32), SIDE, 1).astype(BF16)
    padded[:, :rows] = shifted
    padded[:, rows:] = shifted[:, : 2 * SIDE]
    for step, out in enumerate(outs):
        first = pl.multiple_of(((head + step) & 3) * own, own)
        out[:, :ext] = padded[:, pl.ds(first, ext)]
    fetch_v.wait()
    fetch_o.wait()
    for out in outs:
        for kind in range(3):
            out[:, base + kind * C : base + (kind + 1) * C] = wv[kind]
        out[:, base + 3 * C :] = wo[...]
    for fetch in fetches:
        fetch.wait()


def attend(
    place, c0, c1, c2, c3, far, neighbors, o0, o1, o2, o3, sums,
    bias, xe, dy, wq, wkv, wo, qs, ds, kvt, kv, dkv, dq, att, wflat, dkvt, grads, summed,
    products0, products1, weights0, weights1, means0, means1, qt, dt,
):
    head = place[0]
    own = dy.shape[1]
    ext = own + 2 * SIDE
    full = xe.shape[1]
    border = full - ext
    cand = WINDOW + border
    scale = 1.0 / math.sqrt(HEAD_DIM)
    wq[...] = jnp.zeros_like(wq)
    wo[...] = jnp.zeros_like(wo)
    xe[:, ext:] = far[...].reshape(C, border)
    for step, chunk in enumerate((c0, c1, c2, c3)):
        source = (head - step + 4) & 3
        row = pl.multiple_of(source * 64, 64)
        xe[pl.ds(row, 64), :ext] = chunk[:, :ext]
        dy[pl.ds(row, 64), :] = chunk[:, ext : ext + own]
        base = ext + own
        wflat[pl.ds(row, 64), :] = chunk[:, base : base + C]
        for k in range(2):
            dest = pl.multiple_of(source * 128 + 64 * k, 64)
            part = slice(32 * k, 32 * k + 32)
            wq[pl.ds(dest, 32), :] = chunk[part, base : base + C]
            wkv[pl.ds(dest, 32), :] = chunk[part, base + C : base + 2 * C]
            wkv[pl.ds(dest + 32, 32), :] = chunk[part, base + 2 * C : base + 3 * C]
            wo[pl.ds(dest + 32, 32), :] = chunk[part, base + 3 * C :]
    for start in range(0, full, 256):
        cols = slice(start, start + 256)
        block = nn(wkv[...], xe[:, cols]).astype(BF16)
        kvt[:, cols] = block
        kv[cols, :] = block.T
    for start in range(0, ext, 384):
        cols = slice(start, start + 384)
        qs[cols, :] = nn(wq[...], xe[:, cols]).astype(BF16).T
    for start in range(0, own, 256):
        cols = slice(start, start + 256)
        block = nn(wo[...], dy[:, cols]).astype(BF16)
        dt[:, cols] = block
        ds[cols, :] = block.T
        qt[:, cols] = qs[start + SIDE : start + SIDE + 256, :].T
    dkv[...] = jnp.zeros_like(dkv)
    dq[:, own:] = jnp.zeros((C, 2 * SIDE), F32)
    lane_head = lax.broadcasted_iota(jnp.int32, (BLOCK, C), 1) // 64

    zero = jnp.zeros((BLOCK, C), BF16)
    last = own // BLOCK - 1

    def operands(b, g, hh):
        first = pl.multiple_of(b * BLOCK, BLOCK)
        cols = slice(C * g, C * g + C)
        mine = lane_head == hh
        query = jnp.where(mine, qs[pl.ds(first + SIDE, BLOCK), cols], zero)
        dout = jnp.where(mine, ds[pl.ds(first, BLOCK), cols], zero)
        return jnp.concatenate([query, dout], axis=0)

    def multiply(b, g, hh, products):
        first = pl.multiple_of(b * BLOCK, BLOCK)
        cols = slice(C * g, C * g + C)
        out = slice(C * hh, C * hh + 2 * C)
        stack = jnp.concatenate([operands(b, g, hh), operands(b, g, hh + 1)], axis=0)
        products[:WINDOW, out] = nt(kv[pl.ds(first, WINDOW), cols], stack)
        products[WINDOW:, out] = nt(kv[ext:, cols], stack)

    def first_pass(block, hh, products):
        left = slice(C * hh, C * hh + BLOCK)
        acc = jnp.zeros((PARTS, BLOCK), F32)
        for start in range(0, cand, CHUNK):
            rows = slice(start, start + CHUNK)
            expon = jnp.exp2(products[rows, left] * (scale * LOG2E) + bias[rows, :])
            products[rows, left] = expon
            acc = acc + expon.reshape(CHUNK // PARTS, PARTS, BLOCK).sum(0)
        return 1.0 / jnp.sum(acc, axis=0, keepdims=True)

    def second_pass(hh, products, weights, means, inverse):
        left = slice(C * hh, C * hh + BLOCK)
        right = slice(C * hh + BLOCK, C * hh + C)
        acc = jnp.zeros((PARTS, BLOCK), F32)
        for start in range(0, cand, CHUNK):
            rows = slice(start, start + CHUNK)
            prob = products[rows, left] * inverse
            term = prob * products[rows, right]
            weights[rows, left] = term.astype(BF16)
            weights[rows, right] = prob.astype(BF16)
            acc = acc + term.reshape(CHUNK // PARTS, PARTS, BLOCK).sum(0)
        means[hh : hh + 1, :] = jnp.sum(acc, axis=0, keepdims=True)

    def gather_rows(b, g, hh, weights, means):
        first = pl.multiple_of(b * BLOCK, BLOCK)
        top = C * g + 64 * hh
        pair = jnp.concatenate(
            [kvt[top : top + 64, pl.ds(first, WINDOW)], kvt[top : top + 64, ext:]], axis=1
        )
        result = nn(pair, weights[:, C * hh : C * hh + C])
        grad_query = result[:32, :BLOCK] - result[:32, BLOCK:] * means[hh : hh + 1, :]
        low = 128 * g + 32 * hh
        dq[low : low + 32, pl.ds(first, BLOCK)] = grad_query * scale
        att[low : low + 32, pl.ds(first, BLOCK)] = result[32:, BLOCK:].astype(BF16)

    def spread(b, g, hh, weights, means):
        first = pl.multiple_of(b * BLOCK, BLOCK)
        top = C * g + 64 * hh
        query = qt[top : top + 64, pl.ds(first, BLOCK)]
        dout = dt[top : top + 64, pl.ds(first, BLOCK)]
        second = dout - (query.astype(F32) * means[hh : hh + 1, :]).astype(BF16)
        both = jnp.concatenate([query, second], axis=1)
        cols = slice(C * hh, C * hh + C)
        out = nt(both, weights[:, cols])
        dkv[top : top + 64, pl.ds(first, WINDOW)] += out[:, :WINDOW]
        dkv[top : top + 64, ext:] += out[:, WINDOW:]

    def phase(block, ahead, group, behind, products, weights, means, products_next, weights_done, means_done):
        inv0 = first_pass(block, 0, products)
        multiply(*ahead, 0, products_next)
        second_pass(0, products, weights, means, inv0)
        gather_rows(*behind, 0, weights_done, means_done)
        spread(*behind, 0, weights_done, means_done)
        inv1 = first_pass(block, 1, products)
        second_pass(1, products, weights, means, inv1)
        gather_rows(*behind, 1, weights_done, means_done)
        spread(*behind, 1, weights_done, means_done)
        inv2 = first_pass(block, 2, products)
        multiply(*ahead, 2, products_next)
        second_pass(2, products, weights, means, inv2)
        gather_rows(*behind, 2, weights_done, means_done)
        spread(*behind, 2, weights_done, means_done)
        inv3 = first_pass(block, 3, products)
        second_pass(3, products, weights, means, inv3)
        gather_rows(*behind, 3, weights_done, means_done)
        spread(*behind, 3, weights_done, means_done)

    def step(b, carry):
        near = neighbors[:, pl.ds(pl.multiple_of(head * own + b * BLOCK, BLOCK), BLOCK)]
        shifted = (near - (head * own + b * BLOCK - SIDE)) & (neighbors.shape[1] - 1)
        index = jnp.where(near < neighbors.shape[1], shifted, near - neighbors.shape[1] + WINDOW)
        for start in range(0, cand, CHUNK):
            rows = lax.broadcasted_iota(jnp.int32, (CHUNK, BLOCK), 0) + start
            count = jnp.zeros((CHUNK, BLOCK), F32)
            for slot in range(NBR):
                count = count + jnp.where(rows == index[slot : slot + 1, :], 1.0, 0.0)
            bias[start : start + CHUNK, :] = jnp.where(count > 0.5, jnp.log(count) * LOG2E, -1e30)
        before = jnp.maximum(b - 1, 0)
        after = jnp.minimum(b + 1, last)
        phase(b, (b, 1), 0, (before, 1), products0, weights0, means0, products1, weights1, means1)
        phase(b, (after, 0), 1, (b, 0), products1, weights1, means1, products0, weights0, means0)
        return carry

    weights1[...] = jnp.zeros_like(weights1)
    means0[...] = jnp.zeros_like(means0)
    means1[...] = jnp.zeros_like(means1)
    for hh in (0, 2):
        multiply(0, 0, hh, products0)
    lax.fori_loop(0, own // BLOCK, step, 0)
    for hh in range(4):
        gather_rows(last, 1, hh, weights1, means1)
        spread(last, 1, hh, weights1, means1)
    row_scale = jnp.where((lax.broadcasted_iota(jnp.int32, (2 * C, 128), 0) & 63) < 32, scale, 1.0)
    for start in range(0, full, 128):
        cols = slice(start, start + 128)
        dkvt[:, cols] = (dkv[:, cols] * row_scale).astype(BF16)
    own_grads = pltpu.roll(dq[...], SIDE, 1).astype(BF16)
    summed[:, :ext] = (tn(wkv[...], dkvt[:, :ext]) + tn(wflat[...], own_grads)).astype(BF16)
    summed[:, ext:] = tn(wkv[...], dkvt[:, ext:]).astype(BF16)
    grad_query = nt(own_grads, xe[:, :ext]).astype(BF16)
    grads[...] = nt(dkvt[...], xe[...]).astype(BF16)
    grad_out = nt(att[...], dy[...]).astype(BF16)
    for target in range(4):
        sums[target, :64, :] = grad_query[64 * target : 64 * target + 64, :]
        sums[target, 192:, :] = grad_out[64 * target : 64 * target + 64, :]
        for k in range(2):
            top = 128 * target + 64 * k
            sums[target, 64 + 32 * k : 96 + 32 * k, :] = grads[top : top + 32, :]
            sums[target, 128 + 32 * k : 160 + 32 * k, :] = grads[top + 32 : top + 64, :]
    for step_out, out in enumerate((o0, o1, o2, o3)):
        target = (head + step_out) & 3
        out[...] = summed[pl.ds(pl.multiple_of(target * 64, 64), 64), :]


def add_up(r0, r1, r2, r3, b0, b1, b2):
    border = b0.shape[1]
    first = r0.shape[1] - 3 * border
    for peer, out in enumerate((b0, b1, b2)):
        cols = slice(first + peer * border, first + (peer + 1) * border)
        out[...] = sum(part[:, cols].astype(F32) for part in (r0, r1, r2, r3)).astype(BF16)


def finish(place, r0, r1, r2, r3, b0, b1, b2, grad_in, lists, out, padded):
    head = place[0]
    rows = grad_in.shape[1]
    own = rows // 4
    ext = own + 2 * SIDE
    padded[...] = jnp.zeros_like(padded)
    for step, part in enumerate((r0, r1, r2, r3)):
        source = (head - step + 4) & 3
        first = pl.multiple_of(source * own, own)
        padded[:, pl.ds(first, ext)] += part[:, :ext].astype(F32)
    padded[:, : 2 * SIDE] += padded[:, rows:]
    aligned = pltpu.roll(padded[:, :rows], rows - SIDE, 1)
    back = jnp.concatenate([b0[...], b1[...], b2[...]], axis=1)
    for start in range(0, rows, 512):
        cols = slice(start, start + 512)
        returned = nt(back, one_hot_rows(lists[...], start, 512))
        out[:, cols] = grad_in[:, cols].astype(F32) + aligned[:, cols] + returned


def kernel_call(body, out_shape, inputs, scratch=(), mib=48, loose=()):
    specs = []
    for place, value in enumerate(inputs):
        if value.dtype == jnp.int32 and value.size == 1:
            specs.append(pl.BlockSpec(memory_space=pltpu.SMEM))
        elif place in loose:
            specs.append(pl.BlockSpec(memory_space=pltpu.HBM))
        else:
            specs.append(vmem_spec())
    outs = [vmem_spec() for _ in out_shape] if isinstance(out_shape, (list, tuple)) else vmem_spec()
    return pl.pallas_call(
        body,
        out_shape=out_shape,
        in_specs=specs,
        out_specs=outs,
        scratch_shapes=list(scratch),
        compiler_params=pltpu.CompilerParams(vmem_limit_bytes=mib * 1024 * 1024),
    )(*inputs)


def sds(shape, dtype):
    return jax.ShapeDtypeStruct(shape, dtype)


def attend_call(place, *args):
    *inputs, own, ext, full, cand = args
    return kernel_call(
        attend,
        [sds((64, full), BF16)] * 4 + [sds((4, C, C), BF16)],
        (place, *inputs),
        [
            pltpu.VMEM((cand, BLOCK), F32),
            pltpu.VMEM((C, full), BF16),
            pltpu.VMEM((C, own), BF16),
            pltpu.VMEM((2 * C, C), BF16),
            pltpu.VMEM((2 * C, C), BF16),
            pltpu.VMEM((2 * C, C), BF16),
            pltpu.VMEM((ext, 2 * C), BF16),
            pltpu.VMEM((own, 2 * C), BF16),
            pltpu.VMEM((2 * C, full), BF16),
            pltpu.VMEM((full, 2 * C), BF16),
            pltpu.VMEM((2 * C, full), F32),
            pltpu.VMEM((C, ext), F32),
            pltpu.VMEM((C, own), BF16),
            pltpu.VMEM((C, C), BF16),
            pltpu.VMEM((2 * C, full), BF16),
            pltpu.VMEM((2 * C, C), BF16),
            pltpu.VMEM((C, full), BF16),
            pltpu.VMEM((cand, 4 * C), F32),
            pltpu.VMEM((cand, 4 * C), F32),
            pltpu.VMEM((cand, 4 * C), BF16),
            pltpu.VMEM((cand, 4 * C), BF16),
            pltpu.VMEM((8, BLOCK), F32),
            pltpu.VMEM((8, BLOCK), F32),
            pltpu.VMEM((2 * C, own), BF16),
            pltpu.VMEM((2 * C, own), BF16),
        ],
    )


def local(tokens, grad_in, w_qkv, w_out, neighbors, send_rows):
    groups = lax.axis_size("tile")
    border = send_rows.shape[2]
    offsets = (1, groups - 1, groups // 2)
    rows = tokens.shape[1]
    own = rows // 4
    ext = own + 2 * SIDE
    full = ext + 3 * border
    cand = WINDOW + 3 * border
    place = lax.axis_index("head").reshape(1).astype(jnp.int32)
    lists = send_rows.reshape(1, 3 * border)
    width = ext + own + 4 * C

    with jax.named_scope("border_rows"):
        halo = kernel_call(
            choose,
            sds((64, 3 * border), BF16),
            (tokens, lists),
            [pltpu.VMEM((64, rows), BF16), pltpu.SemaphoreType.DMA((4,))],
            loose=(0,),
        )
    with jax.named_scope("prepare"):
        chunks = kernel_call(
            prepare,
            [sds((64, width), BF16)] * 4,
            (place, tokens, grad_in, w_qkv, w_out, halo),
            [
                pltpu.VMEM((64, rows), BF16),
                pltpu.VMEM((3, 64, C), BF16),
                pltpu.VMEM((64, C), BF16),
                pltpu.VMEM((64, rows + 2 * SIDE), BF16),
                pltpu.SemaphoreType.DMA((7,)),
            ],
            loose=(1, 2, 3, 4),
        )
    with jax.named_scope("border_rows"):
        mine = jnp.concatenate(
            [
                passed_along(halo[:, peer * border : (peer + 1) * border], "tile", offsets[peer])
                for peer in range(3)
            ],
            axis=1,
        )
        spread = lax.all_to_all(
            jnp.broadcast_to(mine[None], (4, 64, 3 * border)), "head", 0, 0
        )
    with jax.named_scope("exchange"):
        chunks = [chunks[0]] + [passed_along(chunks[step], "head", step) for step in (1, 2, 3)]
    with jax.named_scope("attention"):
        *parts, sums = attend_call(place, *chunks, spread, neighbors, own, ext, full, cand)
    with jax.named_scope("return"):
        parts = [parts[0]] + [passed_along(parts[step], "head", step) for step in (1, 2, 3)]
    with jax.named_scope("weight_sums"):
        value = lax.all_to_all(
            sums.reshape(32, C // 8, C), ("tile", "head"), 0, 0, axis_index_groups=plates(4)
        )
        value = value.astype(F32).sum(0).astype(BF16)
        *parts, value = lax.optimization_barrier((*parts, value))
    with jax.named_scope("return"):
        back = kernel_call(add_up, [sds((64, border), BF16)] * 3, tuple(parts))
        back = [
            passed_along(back[peer], "tile", (groups - offsets[peer]) % groups)
            for peer in range(3)
        ]
    with jax.named_scope("weight_sums"):
        line = [[16 * y + 2 * z + c for z in range(8)] for y in range(4) for c in range(2)]
        piece = (8, C // 8, C)
        value = grouped(jnp.broadcast_to(value[None], piece), line)
        grad_scale = 1.0 / math.sqrt(rows * groups)
        value = value.astype(F32).sum(0) * grad_scale
        *back, value = lax.optimization_barrier((*back, value))
        value = grouped(jnp.broadcast_to(value[None], piece), plates(1))
        value = value.reshape(4, 64, C)
    with jax.named_scope("return"):
        d_tokens = kernel_call(
            finish,
            sds((64, rows), F32),
            (place, *parts, *back, grad_in, lists),
            [pltpu.VMEM((64, rows + 2 * SIDE), F32)],
        )
    return (d_tokens, value[:3], value[3])


def solution(mesh):
    return jax.shard_map(
        local,
        mesh=mesh,
        in_specs=(
            P("head", "tile"),
            P("head", "tile"),
            P(None, "head", None),
            P("head", None),
            P(None, "tile"),
            P("tile", None, None),
        ),
        out_specs=(P("head", "tile"), P(None, "head", None), P("head", None)),
        check_vma=False,
    )
```

```python
import math

import jax
import jax.numpy as jnp
from jax import lax
from jax.experimental import pallas as pl
from jax.experimental.pallas import tpu as pltpu
from jax.sharding import PartitionSpec as P

C = 256
HEADS = 8
NBR = 9
HEAD_DIM = 32
BLOCK = 128
SIDE = 64
CHUNK = 64
PARTS = 32
WINDOW = BLOCK + 2 * SIDE
LOG2E = math.log2(math.e)
F32 = jnp.float32
BF16 = jnp.bfloat16


def passed_along(value, axis, steps):
    count = lax.axis_size(axis)
    pairs = [(source, (source + steps) % count) for source in range(count)]
    return lax.ppermute(value, axis, pairs)


def grouped(value, groups):
    return lax.all_to_all(value, "tile", 0, 0, axis_index_groups=groups)


def plates(heads):
    return [
        [(16 * y + 2 * z + c) * heads + h for h in range(heads) for y in range(4) for c in range(2)]
        for z in range(8)
    ]


def vmem_spec():
    return pl.BlockSpec(memory_space=pltpu.VMEM)


def nt(a, b):
    return lax.dot_general(a, b, (((1,), (1,)), ((), ())), preferred_element_type=F32)


def tn(a, b):
    return lax.dot_general(a, b, (((0,), (0,)), ((), ())), preferred_element_type=F32)


def nn(a, b):
    return jnp.dot(a, b, preferred_element_type=F32)


def one_hot_rows(lists, start, count):
    rows = lax.broadcasted_iota(jnp.int32, (count, lists.shape[1]), 0) + start
    return jnp.where(rows == lists, 1.0, 0.0).astype(BF16)


def choose(tokens, lists, halo, x, sems):
    rows = tokens.shape[1]
    quarter = rows // 4
    fetches = [
        pltpu.make_async_copy(
            tokens.at[:, pl.ds(part * quarter, quarter)],
            x.at[:, pl.ds(part * quarter, quarter)],
            sems.at[part],
        )
        for part in range(4)
    ]
    for fetch in fetches:
        fetch.start()
    chosen = jnp.zeros(halo.shape, F32)
    for part, fetch in enumerate(fetches):
        fetch.wait()
        for start in range(part * quarter, (part + 1) * quarter, 512):
            chosen = chosen + nn(x[:, start : start + 512], one_hot_rows(lists[...], start, 512))
    halo[...] = chosen.astype(BF16)


def prepare(
    place, tokens, grad_in, w_qkv, w_out, halo, out0, out1, out2, out3, x, wv, wo, padded, sems
):
    head = place[0]
    rows = tokens.shape[1]
    own = rows // 4
    ext = own + 2 * SIDE
    base = ext + own
    outs = (out0, out1, out2, out3)
    fetch_x = pltpu.make_async_copy(tokens, x, sems.at[0])
    fetch_v = pltpu.make_async_copy(w_qkv, wv, sems.at[1])
    fetch_o = pltpu.make_async_copy(w_out, wo, sems.at[2])
    fetches = [
        pltpu.make_async_copy(
            grad_in.at[:, pl.ds(pl.multiple_of(((head + step) & 3) * own, own), own)],
            out.at[:, pl.ds(ext, own)],
            sems.at[3 + step],
        )
        for step, out in enumerate(outs)
    ]
    fetch_x.start()
    fetch_v.start()
    fetch_o.start()
    for fetch in fetches:
        fetch.start()
    fetch_x.wait()
    shifted = pltpu.roll(x[...].astype(F32), SIDE, 1).astype(BF16)
    padded[:, :rows] = shifted
    padded[:, rows:] = shifted[:, : 2 * SIDE]
    for step, out in enumerate(outs):
        first = pl.multiple_of(((head + step) & 3) * own, own)
        out[:, :ext] = padded[:, pl.ds(first, ext)]
    fetch_v.wait()
    fetch_o.wait()
    for out in outs:
        for kind in range(3):
            out[:, base + kind * C : base + (kind + 1) * C] = wv[kind]
        out[:, base + 3 * C :] = wo[...]
    for fetch in fetches:
        fetch.wait()


def attend(
    place, c0, c1, c2, c3, far, neighbors, o0, o1, o2, o3, sums,
    bias, xe, dy, wq, wkv, wo, qs, ds, kvt, kv, dkv, dq, att, wflat, dkvt, grads, summed,
    products0, products1, weights0, weights1, means0, means1, qt, dt,
):
    head = place[0]
    own = dy.shape[1]
    ext = own + 2 * SIDE
    full = xe.shape[1]
    border = full - ext
    cand = WINDOW + border
    scale = 1.0 / math.sqrt(HEAD_DIM)
    wq[...] = jnp.zeros_like(wq)
    wo[...] = jnp.zeros_like(wo)
    xe[:, ext:] = far[...].reshape(C, border)
    for step, chunk in enumerate((c0, c1, c2, c3)):
        source = (head - step + 4) & 3
        row = pl.multiple_of(source * 64, 64)
        xe[pl.ds(row, 64), :ext] = chunk[:, :ext]
        dy[pl.ds(row, 64), :] = chunk[:, ext : ext + own]
        base = ext + own
        wflat[pl.ds(row, 64), :] = chunk[:, base : base + C]
        for k in range(2):
            dest = pl.multiple_of(source * 128 + 64 * k, 64)
            part = slice(32 * k, 32 * k + 32)
            wq[pl.ds(dest, 32), :] = chunk[part, base : base + C]
            wkv[pl.ds(dest, 32), :] = chunk[part, base + C : base + 2 * C]
            wkv[pl.ds(dest + 32, 32), :] = chunk[part, base + 2 * C : base + 3 * C]
            wo[pl.ds(dest + 32, 32), :] = chunk[part, base + 3 * C :]
    for start in range(0, full, 256):
        cols = slice(start, start + 256)
        block = nn(wkv[...], xe[:, cols]).astype(BF16)
        kvt[:, cols] = block
        kv[cols, :] = block.T
    for start in range(0, ext, 384):
        cols = slice(start, start + 384)
        qs[cols, :] = nn(wq[...], xe[:, cols]).astype(BF16).T
    for start in range(0, own, 256):
        cols = slice(start, start + 256)
        block = nn(wo[...], dy[:, cols]).astype(BF16)
        dt[:, cols] = block
        ds[cols, :] = block.T
        qt[:, cols] = qs[start + SIDE : start + SIDE + 256, :].T
    dkv[...] = jnp.zeros_like(dkv)
    dq[:, own:] = jnp.zeros((C, 2 * SIDE), F32)
    lane_head = lax.broadcasted_iota(jnp.int32, (BLOCK, C), 1) // 64

    zero = jnp.zeros((BLOCK, C), BF16)
    last = own // BLOCK - 1

    def operands(b, g, hh):
        first = pl.multiple_of(b * BLOCK, BLOCK)
        cols = slice(C * g, C * g + C)
        mine = lane_head == hh
        query = jnp.where(mine, qs[pl.ds(first + SIDE, BLOCK), cols], zero)
        dout = jnp.where(mine, ds[pl.ds(first, BLOCK), cols], zero)
        return jnp.concatenate([query, dout], axis=0)

    def multiply(b, g, hh, products):
        first = pl.multiple_of(b * BLOCK, BLOCK)
        cols = slice(C * g, C * g + C)
        out = slice(C * hh, C * hh + 2 * C)
        stack = jnp.concatenate([operands(b, g, hh), operands(b, g, hh + 1)], axis=0)
        products[:WINDOW, out] = nt(kv[pl.ds(first, WINDOW), cols], stack)
        products[WINDOW:, out] = nt(kv[ext:, cols], stack)

    def first_pass(block, hh, products):
        left = slice(C * hh, C * hh + BLOCK)
        acc = jnp.zeros((PARTS, BLOCK), F32)
        for start in range(0, cand, CHUNK):
            rows = slice(start, start + CHUNK)
            expon = jnp.exp2(products[rows, left] * (scale * LOG2E) + bias[rows, :])
            products[rows, left] = expon
            acc = acc + expon.reshape(CHUNK // PARTS, PARTS, BLOCK).sum(0)
        return 1.0 / jnp.sum(acc, axis=0, keepdims=True)

    def second_pass(hh, products, weights, means, inverse):
        left = slice(C * hh, C * hh + BLOCK)
        right = slice(C * hh + BLOCK, C * hh + C)
        acc = jnp.zeros((PARTS, BLOCK), F32)
        for start in range(0, cand, CHUNK):
            rows = slice(start, start + CHUNK)
            prob = products[rows, left] * inverse
            term = prob * products[rows, right]
            weights[rows, left] = term.astype(BF16)
            weights[rows, right] = prob.astype(BF16)
            acc = acc + term.reshape(CHUNK // PARTS, PARTS, BLOCK).sum(0)
        means[hh : hh + 1, :] = jnp.sum(acc, axis=0, keepdims=True)

    def gather_rows(b, g, hh, weights, means):
        first = pl.multiple_of(b * BLOCK, BLOCK)
        top = C * g + 64 * hh
        pair = jnp.concatenate(
            [kvt[top : top + 64, pl.ds(first, WINDOW)], kvt[top : top + 64, ext:]], axis=1
        )
        result = nn(pair, weights[:, C * hh : C * hh + C])
        grad_query = result[:32, :BLOCK] - result[:32, BLOCK:] * means[hh : hh + 1, :]
        low = 128 * g + 32 * hh
        dq[low : low + 32, pl.ds(first, BLOCK)] = grad_query * scale
        att[low : low + 32, pl.ds(first, BLOCK)] = result[32:, BLOCK:].astype(BF16)

    def spread(b, g, hh, weights, means):
        first = pl.multiple_of(b * BLOCK, BLOCK)
        top = C * g + 64 * hh
        query = qt[top : top + 64, pl.ds(first, BLOCK)]
        dout = dt[top : top + 64, pl.ds(first, BLOCK)]
        second = dout - (query.astype(F32) * means[hh : hh + 1, :]).astype(BF16)
        both = jnp.concatenate([query, second], axis=1)
        cols = slice(C * hh, C * hh + C)
        out = nt(both, weights[:, cols])
        dkv[top : top + 64, pl.ds(first, WINDOW)] += out[:, :WINDOW]
        dkv[top : top + 64, ext:] += out[:, WINDOW:]

    def phase(block, ahead, group, behind, products, weights, means, products_next, weights_done, means_done):
        inv0 = first_pass(block, 0, products)
        multiply(*ahead, 0, products_next)
        second_pass(0, products, weights, means, inv0)
        gather_rows(*behind, 0, weights_done, means_done)
        spread(*behind, 0, weights_done, means_done)
        inv1 = first_pass(block, 1, products)
        second_pass(1, products, weights, means, inv1)
        gather_rows(*behind, 1, weights_done, means_done)
        spread(*behind, 1, weights_done, means_done)
        inv2 = first_pass(block, 2, products)
        multiply(*ahead, 2, products_next)
        second_pass(2, products, weights, means, inv2)
        gather_rows(*behind, 2, weights_done, means_done)
        spread(*behind, 2, weights_done, means_done)
        inv3 = first_pass(block, 3, products)
        second_pass(3, products, weights, means, inv3)
        gather_rows(*behind, 3, weights_done, means_done)
        spread(*behind, 3, weights_done, means_done)

    def step(b, carry):
        near = neighbors[:, pl.ds(pl.multiple_of(head * own + b * BLOCK, BLOCK), BLOCK)]
        shifted = (near - (head * own + b * BLOCK - SIDE)) & (neighbors.shape[1] - 1)
        index = jnp.where(near < neighbors.shape[1], shifted, near - neighbors.shape[1] + WINDOW)
        for start in range(0, cand, CHUNK):
            rows = lax.broadcasted_iota(jnp.int32, (CHUNK, BLOCK), 0) + start
            count = jnp.zeros((CHUNK, BLOCK), F32)
            for slot in range(NBR):
                count = count + jnp.where(rows == index[slot : slot + 1, :], 1.0, 0.0)
            bias[start : start + CHUNK, :] = jnp.where(count > 0.5, jnp.log(count) * LOG2E, -1e30)
        before = jnp.maximum(b - 1, 0)
        after = jnp.minimum(b + 1, last)
        phase(b, (b, 1), 0, (before, 1), products0, weights0, means0, products1, weights1, means1)
        phase(b, (after, 0), 1, (b, 0), products1, weights1, means1, products0, weights0, means0)
        return carry

    weights1[...] = jnp.zeros_like(weights1)
    means0[...] = jnp.zeros_like(means0)
    means1[...] = jnp.zeros_like(means1)
    for hh in (0, 2):
        multiply(0, 0, hh, products0)
    lax.fori_loop(0, own // BLOCK, step, 0)
    for hh in range(4):
        gather_rows(last, 1, hh, weights1, means1)
        spread(last, 1, hh, weights1, means1)
    row_scale = jnp.where((lax.broadcasted_iota(jnp.int32, (2 * C, 128), 0) & 63) < 32, scale, 1.0)
    for start in range(0, full, 128):
        cols = slice(start, start + 128)
        dkvt[:, cols] = (dkv[:, cols] * row_scale).astype(BF16)
    own_grads = pltpu.roll(dq[...], SIDE, 1).astype(BF16)
    summed[:, :ext] = (tn(wkv[...], dkvt[:, :ext]) + tn(wflat[...], own_grads)).astype(BF16)
    summed[:, ext:] = tn(wkv[...], dkvt[:, ext:]).astype(BF16)
    grad_query = nt(own_grads, xe[:, :ext]).astype(BF16)
    grads[...] = nt(dkvt[...], xe[...]).astype(BF16)
    grad_out = nt(att[...], dy[...]).astype(BF16)
    for target in range(4):
        sums[target, :64, :] = grad_query[64 * target : 64 * target + 64, :]
        sums[target, 192:, :] = grad_out[64 * target : 64 * target + 64, :]
        for k in range(2):
            top = 128 * target + 64 * k
            sums[target, 64 + 32 * k : 96 + 32 * k, :] = grads[top : top + 32, :]
            sums[target, 128 + 32 * k : 160 + 32 * k, :] = grads[top + 32 : top + 64, :]
    for step_out, out in enumerate((o0, o1, o2, o3)):
        target = (head + step_out) & 3
        out[...] = summed[pl.ds(pl.multiple_of(target * 64, 64), 64), :]


def add_up(r0, r1, r2, r3, b0, b1, b2):
    border = b0.shape[1]
    first = r0.shape[1] - 3 * border
    for peer, out in enumerate((b0, b1, b2)):
        cols = slice(first + peer * border, first + (peer + 1) * border)
        out[...] = sum(part[:, cols].astype(F32) for part in (r0, r1, r2, r3)).astype(BF16)


def finish(place, r0, r1, r2, r3, b0, b1, b2, grad_in, lists, out, padded):
    head = place[0]
    rows = grad_in.shape[1]
    own = rows // 4
    ext = own + 2 * SIDE
    padded[...] = jnp.zeros_like(padded)
    for step, part in enumerate((r0, r1, r2, r3)):
        source = (head - step + 4) & 3
        first = pl.multiple_of(source * own, own)
        padded[:, pl.ds(first, ext)] += part[:, :ext].astype(F32)
    padded[:, : 2 * SIDE] += padded[:, rows:]
    aligned = pltpu.roll(padded[:, :rows], rows - SIDE, 1)
    back = jnp.concatenate([b0[...], b1[...], b2[...]], axis=1)
    for start in range(0, rows, 512):
        cols = slice(start, start + 512)
        returned = nt(back, one_hot_rows(lists[...], start, 512))
        out[:, cols] = grad_in[:, cols].astype(F32) + aligned[:, cols] + returned


def kernel_call(body, out_shape, inputs, scratch=(), mib=48, loose=()):
    specs = []
    for place, value in enumerate(inputs):
        if value.dtype == jnp.int32 and value.size == 1:
            specs.append(pl.BlockSpec(memory_space=pltpu.SMEM))
        elif place in loose:
            specs.append(pl.BlockSpec(memory_space=pltpu.HBM))
        else:
            specs.append(vmem_spec())
    outs = [vmem_spec() for _ in out_shape] if isinstance(out_shape, (list, tuple)) else vmem_spec()
    return pl.pallas_call(
        body,
        out_shape=out_shape,
        in_specs=specs,
        out_specs=outs,
        scratch_shapes=list(scratch),
        compiler_params=pltpu.CompilerParams(vmem_limit_bytes=mib * 1024 * 1024),
    )(*inputs)


def sds(shape, dtype):
    return jax.ShapeDtypeStruct(shape, dtype)


def attend_call(place, *args):
    *inputs, own, ext, full, cand = args
    return kernel_call(
        attend,
        [sds((64, full), BF16)] * 4 + [sds((4, C, C), BF16)],
        (place, *inputs),
        [
            pltpu.VMEM((cand, BLOCK), F32),
            pltpu.VMEM((C, full), BF16),
            pltpu.VMEM((C, own), BF16),
            pltpu.VMEM((2 * C, C), BF16),
            pltpu.VMEM((2 * C, C), BF16),
            pltpu.VMEM((2 * C, C), BF16),
            pltpu.VMEM((ext, 2 * C), BF16),
            pltpu.VMEM((own, 2 * C), BF16),
            pltpu.VMEM((2 * C, full), BF16),
            pltpu.VMEM((full, 2 * C), BF16),
            pltpu.VMEM((2 * C, full), F32),
            pltpu.VMEM((C, ext), F32),
            pltpu.VMEM((C, own), BF16),
            pltpu.VMEM((C, C), BF16),
            pltpu.VMEM((2 * C, full), BF16),
            pltpu.VMEM((2 * C, C), BF16),
            pltpu.VMEM((C, full), BF16),
            pltpu.VMEM((cand, 4 * C), F32),
            pltpu.VMEM((cand, 4 * C), F32),
            pltpu.VMEM((cand, 4 * C), BF16),
            pltpu.VMEM((cand, 4 * C), BF16),
            pltpu.VMEM((8, BLOCK), F32),
            pltpu.VMEM((8, BLOCK), F32),
            pltpu.VMEM((2 * C, own), BF16),
            pltpu.VMEM((2 * C, own), BF16),
        ],
    )


def local(tokens, grad_in, w_qkv, w_out, neighbors, send_rows):
    groups = lax.axis_size("tile")
    border = send_rows.shape[2]
    offsets = (1, groups - 1, groups // 2)
    rows = tokens.shape[1]
    own = rows // 4
    ext = own + 2 * SIDE
    full = ext + 3 * border
    cand = WINDOW + 3 * border
    place = lax.axis_index("head").reshape(1).astype(jnp.int32)
    lists = send_rows.reshape(1, 3 * border)
    width = ext + own + 4 * C

    with jax.named_scope("border_rows"):
        halo = kernel_call(
            choose,
            sds((64, 3 * border), BF16),
            (tokens, lists),
            [pltpu.VMEM((64, rows), BF16), pltpu.SemaphoreType.DMA((4,))],
            loose=(0,),
        )
    with jax.named_scope("prepare"):
        chunks = kernel_call(
            prepare,
            [sds((64, width), BF16)] * 4,
            (place, tokens, grad_in, w_qkv, w_out, halo),
            [
                pltpu.VMEM((64, rows), BF16),
                pltpu.VMEM((3, 64, C), BF16),
                pltpu.VMEM((64, C), BF16),
                pltpu.VMEM((64, rows + 2 * SIDE), BF16),
                pltpu.SemaphoreType.DMA((7,)),
            ],
            loose=(1, 2, 3, 4),
        )
    with jax.named_scope("border_rows"):
        mine = jnp.concatenate(
            [
                passed_along(halo[:, peer * border : (peer + 1) * border], "tile", offsets[peer])
                for peer in range(3)
            ],
            axis=1,
        )
        spread = lax.all_to_all(
            jnp.broadcast_to(mine[None], (4, 64, 3 * border)), "head", 0, 0
        )
    with jax.named_scope("exchange"):
        chunks = [chunks[0]] + [passed_along(chunks[step], "head", step) for step in (1, 2, 3)]
    with jax.named_scope("attention"):
        *parts, sums = attend_call(place, *chunks, spread, neighbors, own, ext, full, cand)
    with jax.named_scope("return"):
        parts = [parts[0]] + [passed_along(parts[step], "head", step) for step in (1, 2, 3)]
    with jax.named_scope("weight_sums"):
        value = lax.all_to_all(
            sums.reshape(32, C // 8, C), ("tile", "head"), 0, 0, axis_index_groups=plates(4)
        )
        value = value.astype(F32).sum(0).astype(BF16)
    with jax.named_scope("weight_sums"):
        line = [[16 * y + 2 * z + c for z in range(8)] for y in range(4) for c in range(2)]
        piece = (8, C // 8, C)
        value = grouped(jnp.broadcast_to(value[None], piece), line)
        grad_scale = 1.0 / math.sqrt(rows * groups)
        value = value.astype(F32).sum(0) * grad_scale
        *parts, value = lax.optimization_barrier((*parts, value))
        value = grouped(jnp.broadcast_to(value[None], piece), plates(1))
        value = value.reshape(4, 64, C)
    with jax.named_scope("return"):
        back = kernel_call(add_up, [sds((64, border), BF16)] * 3, tuple(parts))
        back = [
            passed_along(back[peer], "tile", (groups - offsets[peer]) % groups)
            for peer in range(3)
        ]
    with jax.named_scope("return"):
        d_tokens = kernel_call(
            finish,
            sds((64, rows), F32),
            (place, *parts, *back, grad_in, lists),
            [pltpu.VMEM((64, rows + 2 * SIDE), F32)],
        )
    return (d_tokens, value[:3], value[3])


def solution(mesh):
    return jax.shard_map(
        local,
        mesh=mesh,
        in_specs=(
            P("head", "tile"),
            P("head", "tile"),
            P(None, "head", None),
            P("head", None),
            P(None, "tile"),
            P("tile", None, None),
        ),
        out_specs=(P("head", "tile"), P(None, "head", None), P("head", None)),
        check_vma=False,
    )
```
